256 devices in a mesh: row: 8 (over z), col: 16 (over x_hi, y, core), front: 2 (over x_lo).
Axes of the slice: x: 4 (x_hi: 2, x_lo: 2; x = x_hi * 2 + x_lo), y: 4, z: 8, core: 2. Of those that a mesh axis runs over, the one named last changes fastest.
Arguments:
- front: float32 [2, 6, 2048, 3, 4096], P('front', None, 'row', None, 'col')
- child_update: float32 [2, 2048, 2048], P('front', 'row', 'col'), may hold values from -6 to 6
- child_map: int32 [2, 2048], P('front'), may hold values from 0 to 12287, as said below
- pattern: int32 [2, 48, 48], P('front'), may hold values 0 or 1
Outputs:
- new_front: float32 [2, 6, 2048, 3, 4096], P('front', None, 'row', None, 'col')
The draws below stay inside these ranges and needn't reach their ends.
Inputs may be any that keep to these rules, and one draw needn't show every extreme that they name: `child_map`: entries of one front are distinct. Each aligned run of 128 entries holds exactly 8 entries g with (g // 256) % 16 equal to each index of col.
All inputs are finite; a program needn't handle non-finite values. No bound on the sum of `pattern` on one device may be relied on, other than what follows from the above.
Results may differ from the reference program's by a relative error of at most 0.0001.
Values sent between devices are 32-bit elements; how exact they have to be, the bound alone decides.
No kernel may reach another device: no remote copies, remote signals or barrier semaphores. Data moves between devices by JAX's collectives and lax.ppermute only.
A program may use at most 128 MiB of HBM per device.

```python
import jax
import jax.numpy as jnp
from jax import lax

NF = 12288
BS = 256
PB = 4
NC = 2048
PW = 1024
NB = 48
LR = 6
LC = 3
N_ROW = 8
N_COL = 16


def draw_front(key, part):
    key = jax.random.fold_in(key, 1)
    key_values = jax.random.fold_in(key, 0)
    values = jax.random.normal(key_values, (2, NF, NF), jnp.float32)
    places = jnp.arange(NF, dtype=jnp.int32)
    diagonal = (places[:, None] == places[None, :]).astype(jnp.float32)
    values = values + 8.0 * PW ** 0.5 * diagonal[None]
    return values.reshape(2, LR, N_ROW * BS, LC, N_COL * BS)


def one_child_map(key):
    per_owner = NC // N_COL
    per_slab = NC // (N_COL * N_COL)
    owner_cols = NF // N_COL
    keys = jax.random.split(key, 2 * N_COL)
    chosen = jax.vmap(lambda sub_key: jax.random.permutation(sub_key, owner_cols)[:per_owner])(keys[:N_COL])
    owners = jnp.arange(N_COL, dtype=jnp.int32)[:, None]
    placed = (chosen // BS * N_COL + owners) * BS + chosen % BS
    placed = placed.reshape(N_COL, N_COL, per_slab).transpose(1, 0, 2).reshape(N_COL, N_COL * per_slab)
    shuffles = jax.vmap(lambda sub_key: jax.random.permutation(sub_key, N_COL * per_slab))(keys[N_COL:])
    placed = jnp.take_along_axis(placed, shuffles.astype(jnp.int32), axis=1)
    return placed.reshape(NC).astype(jnp.int32)


def draw_child_map(key, part):
    key = jax.random.fold_in(key, 2)
    keys = jax.random.split(key, 2)
    return jax.vmap(one_child_map)(keys)


def place_ends(drawn, stream_key, least, largest):
    dims = drawn.shape
    place = [jax.random.randint(jax.random.fold_in(stream_key, axis), (), 0, dims[axis]) for axis in range(len(dims))]
    drawn = drawn.at[tuple(place)].set(least)
    longest = dims.index(max(dims))
    place[longest] = (place[longest] + 1) % dims[longest]
    return drawn.at[tuple(place)].set(largest)


def level_of(rng, dims, shards, smallest, largest):
    loudness, own = 1.0, jax.random.fold_in(rng, 6)
    for position, parts in shards:
        steps = jnp.exp(jax.random.uniform(jax.random.fold_in(own, position), (parts,), jnp.float32, smallest / len(shards), largest / len(shards)))
        loudness = loudness * jnp.repeat(steps, dims[position] // parts).reshape([-1 if axis == position else 1 for axis in range(len(dims))])
    return loudness


def centred(rng, shape, deviation, reach, cuts=(), kind=jnp.bfloat16):
    entries = deviation * jax.random.normal(rng, shape, jnp.float32)
    if cuts:
        entries = entries * level_of(rng, shape, cuts, -0.22, 0.18)
    return jnp.clip(entries, -reach, reach).astype(kind)


def setup_inputs(seed: int = 0) -> dict:
    streams_of = jax.random.split(jax.random.key(seed), 5)
    front = draw_front(jax.random.fold_in(streams_of[4], 71), 0)
    child_update = centred(streams_of[1], (2, NC, NC), 1.0, 6.0, ((0, 2), (1, 8), (2, 16)), jnp.float32)
    child_map = draw_child_map(jax.random.fold_in(streams_of[4], 71), 0)
    pattern = place_ends((jax.random.randint(streams_of[3], (2, NB, NB), 0, 2) < 1).astype(jnp.int32), jax.random.fold_in(streams_of[3], 1), 0, 1)
    return dict(front=front, child_update=child_update, child_map=child_map, pattern=pattern)


def one_front(front_tile, update, mapping, blocks_kept):
    full = front_tile.reshape(NF, NF)
    added = full.at[mapping[:, None], mapping[None, :]].add(update)
    corner = added[:PW, :PW]
    factor = jnp.linalg.cholesky(0.5 * (corner + corner.T))
    identity = jnp.eye(PW, dtype=jnp.float32)
    inverse = jax.scipy.linalg.solve_triangular(factor, identity, lower=True)
    panel = jnp.dot(added[:, :PW], inverse.T, precision=lax.Precision.HIGHEST)
    schur = jnp.dot(panel, panel.T, precision=lax.Precision.HIGHEST)
    trailing = jnp.arange(NB) >= PB
    chosen = ((blocks_kept == 1) & trailing[:, None] & trailing[None, :]).astype(jnp.float32)
    result = added.reshape(NB, BS, NB, BS) - schur.reshape(NB, BS, NB, BS) * chosen[:, None, :, None]
    result = result.reshape(NF, NF)
    result = result.at[:, :PW].set(panel)
    return result.reshape(LR, N_ROW * BS, LC, N_COL * BS)

def reference(front, child_update, child_map, pattern):
    results = []
    for which in range(2):
        results.append(one_front(front[which], child_update[which], child_map[which], pattern[which]))
    return jnp.stack(results, axis=0)
```

```python
import functools

import jax
import jax.numpy as jnp
from jax import lax
from jax.experimental import pallas as pl
from jax.experimental.pallas import tpu as pltpu
from jax.sharding import PartitionSpec as P

BS = 256
PB = 4
PW = 1024
KB = 128
F32 = jnp.float32
BF16 = jnp.bfloat16
HIGHEST = lax.Precision.HIGHEST
QUARTER = BS // 4

HOLDER = ((0, 6, 8, 14), (1, 7, 9, 15), (2, 4, 10, 12), (3, 5, 11, 13))
SHIFTS = tuple((dx, dy) for dx in range(2) for dy in range(4))


def nn(a, b, precision=None):
    return lax.dot_general(
        a, b, (((1,), (0,)), ((), ())), precision=precision, preferred_element_type=F32
    )


def nt(a, b, precision=None):
    return lax.dot_general(
        a, b, (((1,), (1,)), ((), ())), precision=precision, preferred_element_type=F32
    )


def iota(shape, dim):
    return lax.broadcasted_iota(jnp.int32, shape, dim)


def split2(x):
    high = x.astype(BF16)
    return high, (x - high.astype(F32)).astype(BF16)


def split3(x):
    high = x.astype(BF16)
    rest = x - high.astype(F32)
    middle = rest.astype(BF16)
    return high, middle, (rest - middle.astype(F32)).astype(BF16)


def pack_kernel(place, map_ref, update_ref, msg_ref, rows_ref, cols_ref, rank_s, class_s):
    row, col = place[0], place[1]
    mapping = map_ref[...]
    owner = (mapping >> 8) & 15
    hot = (iota((16, 16, 128), 1) == owner[:, None, :]).astype(F32)
    before = (iota((128, 128), 0) < iota((128, 128), 1)).astype(BF16)
    counts = nn(hot.reshape(256, 128).astype(BF16), before).reshape(16, 16, 128)
    rank = jnp.sum(hot * counts, axis=1).astype(jnp.int32)
    rank_s[...] = rank
    class_s[...] = owner
    slot = rank * 16 + owner
    col_slot = rank_s[pl.ds(col, 1), :] * 16 + class_s[pl.ds(col, 1), :]
    col_hot = (iota((128, 128), 0) == col_slot).astype(F32)
    moved = nt(col_hot, update_ref[...], HIGHEST)
    row_hot = []
    for run in range(2):
        this = class_s[pl.ds(2 * row + run, 1), :]
        row_slot = (this & 7) * 32 + run * 16 + (this >> 3) * 8 + rank_s[pl.ds(2 * row + run, 1), :]
        row_hot.append((iota((256, 128), 0) == row_slot).astype(F32))
    both = nt(moved, jnp.concatenate(row_hot, axis=1), HIGHEST)
    for j in range(8):
        for r in range(8):
            msg_ref[r * 16:(r + 1) * 16, j * 32:(j + 1) * 32] = both[
                j * 16:(j + 1) * 16, r * 32:(r + 1) * 32
            ]
    parts = jnp.concatenate([mapping >> 7, mapping & 127], axis=0).astype(F32).astype(BF16)
    ordered = jnp.zeros((16, 128), F32)
    for run in range(16):
        run_hot = (iota((128, 128), 0) == slot[run:run + 1, :]).astype(F32).astype(BF16)
        moved_map = nt(parts, run_hot)
        both_parts = moved_map[:16] * 128.0 + moved_map[16:]
        ordered = jnp.where(iota((16, 128), 0) == run, both_parts, ordered)
    ordered = ordered.astype(jnp.int32)
    col_target = (((ordered >> 12) << 8) + (ordered & 255)).astype(F32)
    for j in range(8):
        picked = jnp.sum(
            jnp.where(iota((16, 128), 1) == j * 16 + col, col_target, 0.0), axis=1, keepdims=True
        )
        cols_ref[j * 16:(j + 1) * 16, :] = jnp.broadcast_to(picked, (16, 128)).astype(jnp.int32)
    row_target = ((ordered >> 11) << 8) + (ordered & 255)
    row_parts = jnp.concatenate([row_target >> 7, row_target & 127], axis=0).astype(F32)
    lane = iota((128, 256), 1)
    pick = iota((128, 256), 0) == (lane & 7) * 16 + ((lane >> 3) & 1) * 8 + row
    spread = nn(row_parts.astype(BF16), pick.astype(F32).astype(BF16))
    spread = spread[:16] * 128.0 + spread[16:]
    spread = jnp.where((iota((16, 256), 1) >> 4) == iota((16, 256), 0), spread, 0.0)
    rows_ref[...] = jnp.broadcast_to(jnp.sum(spread, axis=0, keepdims=True), (8, 256)).astype(
        jnp.int32
    )


def pack(place, mapping, update):
    smem = pl.BlockSpec(memory_space=pltpu.SMEM)
    vmem = pl.BlockSpec(memory_space=pltpu.VMEM)
    return pl.pallas_call(
        pack_kernel,
        out_shape=(
            jax.ShapeDtypeStruct((128, 256), F32),
            jax.ShapeDtypeStruct((8, 256), jnp.int32),
            jax.ShapeDtypeStruct((128, 128), jnp.int32),
        ),
        in_specs=[smem, vmem, vmem],
        out_specs=(vmem, vmem, vmem),
        scratch_shapes=[pltpu.VMEM((16, 128), jnp.int32), pltpu.VMEM((16, 128), jnp.int32)],
        name="pack",
    )(place, mapping, update)


def add_kernel(recv_ref, rows_ref, cols_ref, front_ref, out_ref, landed_s):
    step = pl.program_id(0)

    @pl.when(step == 0)
    def _():
        recv = recv_ref[...]
        for j in range(8):
            for r in range(8):
                piece = recv[r * 16:(r + 1) * 16, j * 32:(j + 1) * 32]
                for part, value in enumerate(split3(piece)):
                    landed_s[part, j * 16:(j + 1) * 16, r * 32:(r + 1) * 32] = value.astype(F32)

    row_hot = (iota((BS, 256), 0) + step * BS == rows_ref[0:1, :]).astype(F32).astype(BF16)
    placed = nt(row_hot, landed_s[0].astype(BF16))
    placed = placed + nt(row_hot, landed_s[1].astype(BF16))
    placed = placed + nt(row_hot, landed_s[2].astype(BF16))
    parts = split3(placed)
    for m in range(front_ref.shape[1]):
        col_hot = (cols_ref[:, 0:1] == iota((128, BS), 1) + m * BS).astype(F32).astype(BF16)
        added = nn(parts[0], col_hot) + nn(parts[1], col_hot) + nn(parts[2], col_hot)
        out_ref[0, m] = front_ref[0, m] + added


def extend_add(recv, rows, cols, blocks):
    lr, lc = blocks.shape[:2]
    whole = lambda shape: pl.BlockSpec(shape, lambda l: (0,) * len(shape))
    tile = pl.BlockSpec((1, lc, BS, BS), lambda l: (l, 0, 0, 0))
    return pl.pallas_call(
        add_kernel,
        grid=(lr,),
        out_shape=jax.ShapeDtypeStruct(blocks.shape, F32),
        in_specs=[whole((128, 256)), whole((8, 256)), whole((128, 128)), tile],
        out_specs=tile,
        scratch_shapes=[pltpu.VMEM((3, 128, 256), F32)],
        compiler_params=pltpu.CompilerParams(vmem_limit_bytes=32 << 20),
        name="extend_add",
    )(recv, rows, cols, blocks)


def factor_inverse(block):
    a = [block[8 * s:8 * s + 8, :] for s in range(16)]
    sub, lane = iota((8, 128), 0), iota((8, 128), 1)
    lanes_of = lambda x, j: jnp.broadcast_to(x[:, j:j + 1], (8, 128))
    row_of = lambda x, i: jnp.broadcast_to(x[i:i + 1, :], (8, 128))
    for s in range(16):
        js = [8 * s + q for q in range(8)]
        c = [lanes_of(a[s], j) for j in js]
        strip = a[s]
        rows, mult = [], [[None] * 8 for _ in range(8)]
        pivots = jnp.zeros((8, 128), F32)
        for q in range(8):
            pivot = row_of(c[q], q)
            over = 1.0 / pivot
            pivots = jnp.where(sub == q, pivot, pivots)
            below = jnp.where(sub > q, c[q], 0.0)
            strip = jnp.where(lane == js[q], jnp.where(sub == q, 1.0, 0.0), strip)
            row = row_of(strip, q) * over
            rows.append(jnp.where((lane <= js[q]) | (lane > js[7]), row, 0.0))
            for q2 in range(q + 1, 8):
                m = row_of(c[q2], q) * over
                mult[q][q2] = m
                c[q2] = c[q2] - below * m
            strip = strip - below * row
        a[s] = jnp.where(lane <= sub + 8 * s, strip, 0.0) * lax.rsqrt(pivots)
        kept = (lane < js[0]) | (lane > js[7])
        for t in range(s + 1, 16):
            ct = [lanes_of(a[t], j) for j in js]
            for q in range(8):
                for q2 in range(q + 1, 8):
                    ct[q2] = ct[q2] - ct[q] * mult[q][q2]
            value = jnp.where(kept, a[t], 0.0)
            for q in range(8):
                value = value - ct[q] * rows[q]
            a[t] = value
    return jnp.concatenate(a, axis=0)


def load_pieces(place, mine_ref, other_ref, take):
    core, y, x = place[2], place[3], place[4]
    for k in range(PB):
        for q in range(4):
            holder = HOLDER[k][q]
            dx = (x + 2 - holder // 8) & 1
            dy = (y + 4 - (holder // 2) % 4) & 3
            chip = dx * 4 + dy

            @pl.when(core == k % 2)
            def _():
                take(k, q, mine_ref, chip)

            @pl.when(core != k % 2)
            def _():
                take(k, q, other_ref, chip)


def corner_kernel(place, mine_ref, other_ref, inv_ref, s_ref):
    n, b = PW // KB, KB

    def take(k, q, ref, chip):
        for block in range(PB):
            start = block * BS + q * QUARTER
            inv_ref[start:start + QUARTER, k * BS:(k + 1) * BS] = ref[chip, block]

    load_pieces(place, mine_ref, other_ref, take)
    for i in range(n):
        for j in range(i + 1):
            s_ref[i * b:(i + 1) * b, j * b:(j + 1) * b] = 0.5 * (
                inv_ref[i * b:(i + 1) * b, j * b:(j + 1) * b]
                + inv_ref[j * b:(j + 1) * b, i * b:(i + 1) * b].T
            )
    for k in range(n):
        lo, hi = k * b, (k + 1) * b
        diag = factor_inverse(s_ref[lo:hi, lo:hi])
        if k < n - 1:
            below = nt(s_ref[hi:, lo:hi], diag, HIGHEST)
            s_ref[hi:, hi:hi + b] = s_ref[hi:, hi:hi + b] - nt(below, below[:b], HIGHEST)
        if k > 0:
            left = nn(diag, inv_ref[lo:hi, :lo], HIGHEST)
            inv_ref[lo:hi, :lo] = left
        inv_ref[lo:hi, lo:hi] = diag
        if k < n - 1:
            inv_ref[lo:hi, hi:] = jnp.zeros((b, PW - hi), F32)
            for j in range(k + 2, n):
                at = (j - k - 1) * b
                s_ref[j * b:, j * b:(j + 1) * b] = s_ref[j * b:, j * b:(j + 1) * b] - nt(
                    below[at:], below[at:at + b], HIGHEST
                )
            if k > 0:
                inv_ref[hi:, :lo] = inv_ref[hi:, :lo] - nn(below, left, HIGHEST)
            inv_ref[hi:, lo:hi] = -nn(below, diag, HIGHEST)


def corner_inverse(place, mine, other):
    smem = pl.BlockSpec(memory_space=pltpu.SMEM)
    vmem = pl.BlockSpec(memory_space=pltpu.VMEM)
    return pl.pallas_call(
        corner_kernel,
        out_shape=jax.ShapeDtypeStruct((PW, PW), F32),
        in_specs=[smem, vmem, vmem],
        out_specs=vmem,
        scratch_shapes=[pltpu.VMEM((PW, PW), F32)],
        compiler_params=pltpu.CompilerParams(vmem_limit_bytes=48 << 20),
        cost_estimate=pl.CostEstimate(flops=24_000_000_000, bytes_accessed=8 << 20, transcendentals=0),
        name="corner_inverse",
    )(place, mine, other)


def three_pass(a, b):
    return nt(a[0], b[0]) + nt(a[0], b[1]) + nt(a[1], b[0])


def schur_kernel(
    place, pattern, inv_ref, mine_ref, other_ref, cols_ref, e_ref, out_ref,
    inv_h, inv_l, raw_s, col_h, col_l, row_h, row_l, row_f,
):
    row, col = place[0], place[1]
    step = pl.program_id(0)
    lc = e_ref.shape[1]

    def solve(store):
        raw = split2(raw_s[...])
        for j in range(PB):
            deep = (j + 1) * BS
            value = three_pass(
                (raw[0][:, :deep], raw[1][:, :deep]),
                (inv_h[j * BS:deep, :deep], inv_l[j * BS:deep, :deep]),
            )
            store(j, value)

    @pl.when(step == 0)
    def _():
        for j in range(PB):
            high, low = split2(inv_ref[j * BS:(j + 1) * BS, :])
            inv_h[j * BS:(j + 1) * BS, :] = high
            inv_l[j * BS:(j + 1) * BS, :] = low
        for m in range(lc):
            for k in range(PB):
                for q in range(4):
                    for r in range(8):
                        start = q * QUARTER + r * 8
                        raw_s[start:start + 8, k * BS:(k + 1) * BS] = cols_ref[r, HOLDER[k][q], m]

            def store_col(j, value, m=m):
                high, low = split2(value)
                col_h[m, :, j * BS:(j + 1) * BS] = high
                col_l[m, :, j * BS:(j + 1) * BS] = low

            solve(store_col)

    def take(k, q, ref, chip):
        raw_s[q * QUARTER:(q + 1) * QUARTER, k * BS:(k + 1) * BS] = ref[chip, 0]

    load_pieces(place, mine_ref, other_ref, take)

    def store_row(j, value):
        high, low = split2(value)
        row_f[:, j * BS:(j + 1) * BS] = value
        row_h[:, j * BS:(j + 1) * BS] = high
        row_l[:, j * BS:(j + 1) * BS] = low

    solve(store_row)
    block_row = step * 8 + row
    for m in range(lc):
        block_col = m * 16 + col
        applied = (pattern[block_row, block_col] == 1) & (block_row >= PB) & (block_col >= PB)

        @pl.when(applied)
        def _():
            product = three_pass((row_h[...], row_l[...]), (col_h[m], col_l[m]))
            out_ref[0, m] = e_ref[0, m] - product

        @pl.when(jnp.logical_not(applied))
        def _():
            out_ref[0, m] = e_ref[0, m]

    @pl.when(col < PB)
    def _():
        start = pl.multiple_of(jnp.minimum(col, PB - 1) * BS, BS)
        out_ref[0, 0] = row_f[:, pl.ds(start, BS)]


def schur_update(place, pattern, inverse, mine, other, cols, e):
    lr, lc = e.shape[:2]
    smem = pl.BlockSpec(memory_space=pltpu.SMEM)
    whole = lambda shape: pl.BlockSpec(shape, lambda l: (0,) * len(shape))
    piece = pl.BlockSpec((8, 1, QUARTER, BS), lambda l: (0, l, 0, 0))
    tile = pl.BlockSpec((1, lc, BS, BS), lambda l: (l, 0, 0, 0))
    return pl.pallas_call(
        schur_kernel,
        grid=(lr,),
        out_shape=jax.ShapeDtypeStruct(e.shape, F32),
        in_specs=[smem, smem, whole(inverse.shape), piece, piece, whole(cols.shape), tile],
        out_specs=tile,
        scratch_shapes=[
            pltpu.VMEM((PW, PW), BF16),
            pltpu.VMEM((PW, PW), BF16),
            pltpu.VMEM((BS, PW), F32),
            pltpu.VMEM((lc, BS, PW), BF16),
            pltpu.VMEM((lc, BS, PW), BF16),
            pltpu.VMEM((BS, PW), BF16),
            pltpu.VMEM((BS, PW), BF16),
            pltpu.VMEM((BS, PW), F32),
        ],
        compiler_params=pltpu.CompilerParams(vmem_limit_bytes=48 << 20),
        cost_estimate=pl.CostEstimate(flops=16_000_000_000, bytes_accessed=24 << 20, transcendentals=0),
        name="schur_update",
    )(place, pattern, inverse, mine, other, cols, e)


def scatter_quarters(quarters, col):
    got = jnp.where(col < PB, quarters[0], 0.0)
    for q in range(1, 4):
        got = got + lax.ppermute(quarters[q], "col", [(k, HOLDER[k][q]) for k in range(PB)])
    return got


def gather_plane(piece):
    got = []
    for dx, dy in SHIFTS:
        if dx == 0 and dy == 0:
            got.append(piece)
            continue
        pairs = []
        for c in range(16):
            x, y, core = c // 8, (c // 2) % 4, c % 2
            pairs.append((c, ((x + dx) % 2) * 8 + ((y + dy) % 4) * 2 + core))
        got.append(lax.ppermute(piece, "col", pairs))
    mine = jnp.stack(got)
    other = lax.ppermute(mine, "col", [(c, c ^ 1) for c in range(16)])
    return mine, other


def per_device(front, child_update, child_map, pattern):
    row = lax.axis_index("row")
    col = lax.axis_index("col")
    place = jnp.stack([row, col, col % 2, (col // 2) % 4, col // 8]).astype(jnp.int32)
    blocks = front[0].transpose(0, 2, 1, 3)
    lr, lc = blocks.shape[:2]
    msg, rows, cols = pack(place, child_map[0].reshape(16, 128), child_update[0])
    recv = lax.all_to_all(
        msg.reshape(128, 1, 256), ("row", "col"), split_axis=0, concat_axis=0, tiled=True
    ).reshape(128, 256)
    e = extend_add(recv, rows, cols, blocks)

    lead = e[:, 0].reshape(lr, 4, QUARTER, BS)
    corner = scatter_quarters([lead[0, q] for q in range(4)], col)
    shifted = [corner]
    for d in range(1, 8):
        shifted.append(lax.ppermute(corner, "row", [(z, (z + d) % 8) for z in range(PB)]))
    shifted = jnp.stack(shifted)
    corner = jnp.stack(
        [lax.dynamic_index_in_dim(shifted, (row - s) % 8, 0, keepdims=False) for s in range(PB)]
    )
    corner_mine, corner_other = gather_plane(corner)
    inverse = corner_inverse(place, corner_mine, corner_other)

    panel = scatter_quarters([lead[:, q] for q in range(4)], col)
    panel_mine, panel_other = gather_plane(panel)
    sent = panel.reshape(lr, 8, 8, BS).transpose(1, 0, 2, 3)
    sent = lax.all_to_all(sent, "row", split_axis=0, concat_axis=0, tiled=True)
    sent = sent.reshape(8, lc, 2, 8, BS).transpose(2, 0, 1, 3, 4).reshape(16, lc, 8, BS)
    sent = lax.all_to_all(sent, "col", split_axis=0, concat_axis=0, tiled=True)
    held = lax.all_gather(sent, "row", axis=0, tiled=False)

    out = schur_update(place, pattern[0], inverse, panel_mine, panel_other, held, e)
    return out.transpose(0, 2, 1, 3)[None]


def solution(mesh):
    placed = (
        P("front", None, "row", None, "col"),
        P("front", "row", "col"),
        P("front", None),
        P("front", None, None),
    )
    return jax.shard_map(
        per_device,
        mesh=mesh,
        in_specs=placed,
        out_specs=P("front", None, "row", None, "col"),
        check_vma=False,
    )
```

```python
import functools

import jax
import jax.numpy as jnp
from jax import lax
from jax.experimental import pallas as pl
from jax.experimental.pallas import tpu as pltpu
from jax.sharding import PartitionSpec as P

BS = 256
PB = 4
PW = 1024
KB = 128
F32 = jnp.float32
BF16 = jnp.bfloat16
HIGHEST = lax.Precision.HIGHEST
QUARTER = BS // 4

HOLDER = ((0, 6, 8, 14), (1, 7, 9, 15), (2, 4, 10, 12), (3, 5, 11, 13))
CORNER_SHIFTS = (
    (0, 0, 0, 0), (1, 0, 0, 1), (0, 1, 1, 0), (1, 1, 1, 1),
    (0, 3, 2, 0), (1, 3, 2, 1), (0, 2, 3, None), (1, 2, 4, None),
)
PANEL_SHIFTS = tuple((dx, dy, dy, dx) for dy in range(4) for dx in range(2))


def nn(a, b, precision=None):
    return lax.dot_general(
        a, b, (((1,), (0,)), ((), ())), precision=precision, preferred_element_type=F32
    )


def nt(a, b, precision=None):
    return lax.dot_general(
        a, b, (((1,), (1,)), ((), ())), precision=precision, preferred_element_type=F32
    )


def iota(shape, dim):
    return lax.broadcasted_iota(jnp.int32, shape, dim)


def split2(x):
    high = x.astype(BF16)
    return high, (x - high.astype(F32)).astype(BF16)


def split3(x):
    high = x.astype(BF16)
    rest = x - high.astype(F32)
    middle = rest.astype(BF16)
    return high, middle, (rest - middle.astype(F32)).astype(BF16)


def pack_kernel(
    place, map_ref, update_ref, msg_ref, corner_ref, part_ref,
    rows_ref, cols_ref, lanes_ref, panel_ref, panel_lanes_ref, rank_s, class_s, turned_s,
):
    row, col = place[0], place[1]
    mapping = map_ref[...]
    owner = (mapping >> 8) & 15
    hot = (iota((16, 16, 128), 1) == owner[:, None, :]).astype(F32)
    before = (iota((128, 128), 0) < iota((128, 128), 1)).astype(F32).astype(BF16)
    counts = nn(hot.reshape(256, 128).astype(BF16), before).reshape(16, 16, 128)
    rank = jnp.sum(hot * counts, axis=1).astype(jnp.int32)
    rank_s[...] = rank
    class_s[...] = owner
    slot = owner * 8 + rank
    col_slot = class_s[pl.ds(col, 1), :] * 8 + rank_s[pl.ds(col, 1), :]
    col_hot = (iota((128, 128), 0) == col_slot).astype(F32)
    row_hot = []
    for run in range(2):
        this = class_s[pl.ds(2 * row + run, 1), :]
        row_slot = (this & 7) * 32 + run * 16 + (this >> 3) * 8 + rank_s[pl.ds(2 * row + run, 1), :]
        row_hot.append((iota((256, 128), 0) == row_slot).astype(F32))
    moved = nt(update_ref[...], col_hot, HIGHEST)
    moved = nn(jnp.concatenate(row_hot, axis=1), moved, HIGHEST)
    part_ref[...] = jnp.zeros((16, 8, 256), F32)
    for r in range(8):
        for half in range(2):
            msg_ref[r, :, half * 128:(half + 1) * 128] = moved[
                r * 32 + half * 16:r * 32 + half * 16 + 16, :
            ]
        for run in range(2):
            for upper in range(2):
                at = r * 32 + run * 16 + upper * 8
                piece = moved[at:at + 8, 0:32]
                if upper == 0 and r < PB:
                    g = run * 4 + r
                    corner_ref[:, g * 32:(g + 1) * 32] = piece
                for slot_lane in range(4):

                    @pl.when((col & 3) == slot_lane)
                    def _():
                        lo = run * 128 + slot_lane * 32
                        part_ref[upper * 8 + r, :, lo:lo + 32] = piece

    parts = jnp.concatenate([mapping >> 7, mapping & 127], axis=0).astype(F32).astype(BF16)
    ordered = jnp.zeros((16, 128), F32)
    for run in range(16):
        run_hot = (iota((128, 128), 0) == slot[run:run + 1, :]).astype(F32).astype(BF16)
        moved_map = nt(parts, run_hot)
        both_parts = moved_map[:16] * 128.0 + moved_map[16:]
        ordered = jnp.where(iota((16, 128), 0) == run, both_parts, ordered)
    turned_s[...] = jnp.concatenate([ordered, jnp.zeros((112, 128), F32)], axis=0).T
    mine = turned_s[pl.ds(pl.multiple_of(col * 8, 8), 8), :]
    lead = turned_s[0:32, :]
    for run in range(16):
        cols_ref[run * 8:(run + 1) * 8, :] = jnp.broadcast_to(
            mine[:, run:run + 1], (8, 128)
        ).astype(jnp.int32)
        panel_ref[run * 32:(run + 1) * 32, :] = jnp.broadcast_to(
            lead[:, run:run + 1], (32, 128)
        ).astype(jnp.int32)
    whole = ordered.astype(jnp.int32)
    parts = jnp.concatenate([whole >> 7, whole & 127], axis=0).astype(F32).astype(BF16)

    def spread(ref, width, slot_of, run_of):
        lane = iota((128, width), 1)
        pick = (iota((128, width), 0) == slot_of(lane)).astype(F32).astype(BF16)
        value = nn(parts, pick)
        value = value[:16] * 128.0 + value[16:]
        value = jnp.where(run_of(iota((16, width), 1)) == iota((16, width), 0), value, 0.0)
        ref[...] = jnp.broadcast_to(jnp.sum(value, axis=0, keepdims=True), (8, width)).astype(
            jnp.int32
        )

    spread(rows_ref, 256, lambda n: (((n >> 3) & 1) * 8 + row) * 8 + (n & 7), lambda n: n >> 4)
    spread(lanes_ref, 128, lambda n: col * 8 + (n & 7), lambda n: n >> 3)
    spread(panel_lanes_ref, 512, lambda n: n & 31, lambda n: n >> 5)


def pack(place, mapping, update):
    smem = pl.BlockSpec(memory_space=pltpu.SMEM)
    vmem = pl.BlockSpec(memory_space=pltpu.VMEM)
    ints = lambda *shape: jax.ShapeDtypeStruct(shape, jnp.int32)
    return pl.pallas_call(
        pack_kernel,
        out_shape=(
            jax.ShapeDtypeStruct((8, 16, 256), F32),
            jax.ShapeDtypeStruct((8, 256), F32),
            jax.ShapeDtypeStruct((16, 8, 256), F32),
            ints(8, 256),
            ints(128, 128),
            ints(8, 128),
            ints(512, 128),
            ints(8, 512),
        ),
        in_specs=[smem, vmem, vmem],
        out_specs=(vmem,) * 8,
        scratch_shapes=[
            pltpu.VMEM((16, 128), jnp.int32),
            pltpu.VMEM((16, 128), jnp.int32),
            pltpu.VMEM((128, 128), F32),
        ],
        name="pack",
    )(place, mapping, update)


def turn_kernel(recv_ref, out_ref):
    pieces = []
    for r in range(8):
        pieces += [recv_ref[r, :, 0:128], recv_ref[r, :, 128:256]]
    out_ref[...] = jnp.concatenate(pieces, axis=0).T


def turn(recv):
    vmem = pl.BlockSpec(memory_space=pltpu.VMEM)
    return pl.pallas_call(
        turn_kernel,
        out_shape=jax.ShapeDtypeStruct((128, 256), F32),
        in_specs=[vmem],
        out_specs=vmem,
        name="turn",
    )(recv)


def row_place(g):
    return ((g >> 11) << 8) + (g & 255)


def col_place(g):
    return ((g >> 12) << 8) + (g & 255)


def as_hot(mask):
    return mask.astype(F32).astype(BF16)


def add_kernel(landed_ref, rows_ref, cols_ref, front_ref, out_ref):
    step = pl.program_id(0)
    row_hot = as_hot(iota((BS, 256), 0) + step * BS == row_place(rows_ref[0:1, :]))
    placed = sum(nt(row_hot, part) for part in split3(landed_ref[...]))
    parts = split3(placed)
    for m in range(front_ref.shape[1]):
        col_hot = as_hot(col_place(cols_ref[:, 0:1]) == iota((128, BS), 1) + m * BS)
        out_ref[0, m] = front_ref[0, m] + sum(nn(part, col_hot) for part in parts)


def extend_add(landed, rows, cols, blocks):
    lr, lc = blocks.shape[:2]
    whole = lambda shape: pl.BlockSpec(shape, lambda l: (0,) * len(shape))
    tile = pl.BlockSpec((1, lc, BS, BS), lambda l: (l, 0, 0, 0))
    return pl.pallas_call(
        add_kernel,
        grid=(lr,),
        out_shape=jax.ShapeDtypeStruct(blocks.shape, F32),
        in_specs=[whole((128, 256)), whole((8, 256)), whole((128, 128)), tile],
        out_specs=tile,
        compiler_params=pltpu.CompilerParams(vmem_limit_bytes=32 << 20),
        cost_estimate=pl.CostEstimate(
            flops=2_000_000_000, bytes_accessed=10 << 20, transcendentals=0
        ),
        name="extend_add",
    )(landed, rows, cols, blocks)


def factor_inverse(block):
    a = [block[8 * s:8 * s + 8, :] for s in range(16)]
    sub, lane = iota((8, 128), 0), iota((8, 128), 1)
    lanes_of = lambda x, j: jnp.broadcast_to(x[:, j:j + 1], (8, 128))
    row_of = lambda x, i: jnp.broadcast_to(x[i:i + 1, :], (8, 128))
    for s in range(16):
        js = [8 * s + q for q in range(8)]
        c = [lanes_of(a[s], j) for j in js]
        strip = a[s]
        rows, mult = [], [[None] * 8 for _ in range(8)]
        pivots = jnp.zeros((8, 128), F32)
        for q in range(8):
            pivot = row_of(c[q], q)
            over = 1.0 / pivot
            pivots = jnp.where(sub == q, pivot, pivots)
            below = jnp.where(sub > q, c[q], 0.0)
            strip = jnp.where(lane == js[q], jnp.where(sub == q, 1.0, 0.0), strip)
            row = row_of(strip, q) * over
            rows.append(jnp.where((lane <= js[q]) | (lane > js[7]), row, 0.0))
            for q2 in range(q + 1, 8):
                m = row_of(c[q2], q) * over
                mult[q][q2] = m
                c[q2] = c[q2] - below * m
            strip = strip - below * row
        a[s] = jnp.where(lane <= sub + 8 * s, strip, 0.0) * lax.rsqrt(pivots)
        kept = (lane < js[0]) | (lane > js[7])
        for t in range(s + 1, 16):
            ct = [lanes_of(a[t], j) for j in js]
            for q in range(8):
                for q2 in range(q + 1, 8):
                    ct[q2] = ct[q2] - ct[q] * mult[q][q2]
            value = jnp.where(kept, a[t], 0.0)
            for q in range(8):
                value = value - ct[q] * rows[q]
            a[t] = value
    return jnp.concatenate(a, axis=0)


def holders(place, mine, other, shifts):
    core, y, x = place[2], place[3], place[4]
    for refs, at_core in ((mine, core), (other, 1 - core)):
        for dx, dy, index, part in shifts:
            ref = refs[index] if part is None else refs[index].at[part]
            from_x, from_y = (x - dx) & 1, (y - dy) & 3
            middle = ((from_y + 1) >> 1) & 1
            yield ref, from_x * 8 + from_y * 2 + at_core, at_core + 2 * middle, from_x * 2 + (from_y >> 1)


def corner_kernel(place, panel_ref, lanes_ref, *refs):
    mine, other = refs[:5], refs[5:10]
    inv_ref, s_ref, raw_s, child_s, placed_s = refs[10:]
    n, b = PW // KB, KB
    row = place[0]
    slot_of = iota((8, 128), 1) >> 5
    for ref, holder, k, q in holders(place, mine, other, CORNER_SHIFTS):
        for block in range(PB):
            start = pl.multiple_of(block * BS + q * QUARTER, QUARTER)
            raw_s[k, pl.ds(start, QUARTER), :] = ref[(row - block) & 3, 0:QUARTER, :]
        lane_slot = holder & 3
        for block in range(2 * PB):
            at = QUARTER + (block // PB) * 8
            for half in range(2):
                value = ref[(row - block) & 3, at:at + 8, half * 128:(half + 1) * 128]
                for g in range(4):
                    start = (block * 2 + half) * 32 + g * 8
                    shifted = pltpu.roll(value, ((lane_slot - g) & 3) * 32, 1)
                    old = child_s[holder >> 2, start:start + 8, :]
                    child_s[holder >> 2, start:start + 8, :] = jnp.where(
                        slot_of == lane_slot, shifted, old
                    )
    child = jnp.concatenate([child_s[i] for i in range(4)], axis=1)
    child = 0.5 * (child + child.T)
    col_hot = as_hot(panel_ref[:, 0:1] == iota((512, PW), 1))
    placed_s[...] = sum(nn(part, col_hot) for part in split3(child))
    lanes = lanes_ref[0:1, :]
    raw = lambda i, j: raw_s[j // 2, i * b:(i + 1) * b, (j % 2) * b:(j % 2 + 1) * b]
    for i in range(n):
        row_hot = as_hot(iota((b, 512), 0) + i * b == lanes)
        added = sum(nn(row_hot, part) for part in split3(placed_s[:, :(i + 1) * b]))
        for j in range(i + 1):
            s_ref[i * b:(i + 1) * b, j * b:(j + 1) * b] = (
                0.5 * (raw(i, j) + raw(j, i).T) + added[:, j * b:(j + 1) * b]
            )
    for k in range(n):
        lo, hi = k * b, (k + 1) * b
        diag = factor_inverse(s_ref[lo:hi, lo:hi])
        if k < n - 1:
            below = nt(s_ref[hi:, lo:hi], diag, HIGHEST)
            s_ref[hi:, hi:hi + b] = s_ref[hi:, hi:hi + b] - nt(below, below[:b], HIGHEST)
        if k > 0:
            left = nn(diag, inv_ref[lo:hi, :lo], HIGHEST)
            inv_ref[lo:hi, :lo] = left
        inv_ref[lo:hi, lo:hi] = diag
        if k < n - 1:
            inv_ref[lo:hi, hi:] = jnp.zeros((b, PW - hi), F32)
            for j in range(k + 2, n):
                at = (j - k - 1) * b
                s_ref[j * b:, j * b:(j + 1) * b] = s_ref[j * b:, j * b:(j + 1) * b] - nt(
                    below[at:], below[at:at + b], HIGHEST
                )
            if k > 0:
                inv_ref[hi:, :lo] = inv_ref[hi:, :lo] - nn(below, left, HIGHEST)
            inv_ref[hi:, lo:hi] = -nn(below, diag, HIGHEST)


def corner_inverse(place, panel, lanes, mine, other):
    smem = pl.BlockSpec(memory_space=pltpu.SMEM)
    vmem = pl.BlockSpec(memory_space=pltpu.VMEM)
    return pl.pallas_call(
        corner_kernel,
        out_shape=jax.ShapeDtypeStruct((PW, PW), F32),
        in_specs=[smem] + [vmem] * 12,
        out_specs=vmem,
        scratch_shapes=[
            pltpu.VMEM((PW, PW), F32),
            pltpu.VMEM((PB, PW, BS), F32),
            pltpu.VMEM((4, 512, 128), F32),
            pltpu.VMEM((512, PW), F32),
        ],
        compiler_params=pltpu.CompilerParams(vmem_limit_bytes=48 << 20),
        cost_estimate=pl.CostEstimate(
            flops=40_000_000_000, bytes_accessed=8 << 20, transcendentals=0
        ),
        name="corner_inverse",
    )(place, panel, lanes, *mine, *other)


def three_pass(a, b):
    return nt(a[0], b[0]) + nt(a[0], b[1]) + nt(a[1], b[0])


def schur_kernel(place, pattern, inv_ref, rows_ref, lanes_ref, panel_ref, held_ref, e_ref, *refs):
    mine, other = refs[:4], refs[4:8]
    (out_ref, inv_h, inv_l, raw_s, col_h, col_l, row_h, row_l, row_f, child_s, child_p) = refs[8:]
    row, col = place[0], place[1]
    step = pl.program_id(0)
    lc = e_ref.shape[1]

    def solve(raw, store):
        raw = split2(raw)
        for j in range(PB):
            deep = (j + 1) * BS
            value = three_pass(
                (raw[0][:, :deep], raw[1][:, :deep]),
                (inv_h[j * BS:deep, :deep], inv_l[j * BS:deep, :deep]),
            )
            store(j, value)

    @pl.when(step == 0)
    def _():
        for j in range(PB):
            high, low = split2(inv_ref[j * BS:(j + 1) * BS, :])
            inv_h[j * BS:(j + 1) * BS, :] = high
            inv_l[j * BS:(j + 1) * BS, :] = low
        col_hot = as_hot(panel_ref[:, 0:1] == iota((512, PW), 1))
        held_child = []
        for run in range(16):
            held_child.append(
                jnp.concatenate(
                    [
                        held_ref[run // 2, 384 + g * 8:392 + g * 8, (run % 2) * 128:(run % 2 + 1) * 128]
                        for g in range(4)
                    ],
                    axis=1,
                )
            )
        held_child = jnp.concatenate(held_child, axis=0)
        placed = split3(sum(nn(part, col_hot) for part in split3(held_child)))
        for m in range(lc):
            raw = []
            for k in range(PB):
                column = []
                for q in range(4):
                    at = HOLDER[k][q] * 24 + m * 8
                    column += [held_ref[r, at:at + 8, :] for r in range(8)]
                raw.append(jnp.concatenate(column, axis=0))
            raw = jnp.concatenate(raw, axis=1)
            row_hot = as_hot(iota((BS, 128), 0) + m * BS == col_place(lanes_ref[0:1, :]))
            raw = raw + sum(nn(row_hot, part) for part in placed)

            def store_col(j, value, m=m):
                high, low = split2(value)
                col_h[m, :, j * BS:(j + 1) * BS] = high
                col_l[m, :, j * BS:(j + 1) * BS] = low

            solve(raw, store_col)
        for ref, holder, k, q in holders(place, mine, other, PANEL_SHIFTS):
            child_s[pl.ds(pl.multiple_of(holder * 32, 32), 32), :] = ref[384:416, :]
        placed = sum(nn(part, col_hot) for part in split3(child_s[...].T))
        for index, part in enumerate(split3(placed)):
            child_p[index] = part

    for ref, holder, k, q in holders(place, mine, other, PANEL_SHIFTS):
        start = pl.multiple_of(q * QUARTER, QUARTER)
        at = pl.multiple_of(step * QUARTER, QUARTER)
        raw_s[k, pl.ds(start, QUARTER), :] = ref[pl.ds(at, QUARTER), :]
    row_hot = as_hot(iota((BS, 256), 0) + step * BS == row_place(rows_ref[0:1, :]))
    raw_rows = jnp.concatenate([raw_s[k] for k in range(PB)], axis=1)
    raw_rows = raw_rows + sum(nn(row_hot, child_p[index]) for index in range(3))

    def store_row(j, value):
        high, low = split2(value)
        row_f[:, j * BS:(j + 1) * BS] = value
        row_h[:, j * BS:(j + 1) * BS] = high
        row_l[:, j * BS:(j + 1) * BS] = low

    solve(raw_rows, store_row)
    block_row = step * 8 + row
    for m in range(lc):
        block_col = m * 16 + col
        applied = (pattern[block_row, block_col] == 1) & (block_row >= PB) & (block_col >= PB)

        @pl.when(applied)
        def _():
            product = three_pass((row_h[...], row_l[...]), (col_h[m], col_l[m]))
            out_ref[0, m] = e_ref[0, m] - product

        @pl.when(jnp.logical_not(applied))
        def _():
            out_ref[0, m] = e_ref[0, m]

    @pl.when(col < PB)
    def _():
        start = pl.multiple_of(jnp.minimum(col, PB - 1) * BS, BS)
        out_ref[0, 0] = row_f[:, pl.ds(start, BS)]


def schur_update(place, pattern, inverse, rows, lanes, panel, held, e, mine, other):
    lr, lc = e.shape[:2]
    smem = pl.BlockSpec(memory_space=pltpu.SMEM)
    whole = lambda x: pl.BlockSpec(x.shape, lambda l: (0,) * x.ndim)
    tile = pl.BlockSpec((1, lc, BS, BS), lambda l: (l, 0, 0, 0))
    return pl.pallas_call(
        schur_kernel,
        grid=(lr,),
        out_shape=jax.ShapeDtypeStruct(e.shape, F32),
        in_specs=[smem, smem]
        + [whole(x) for x in (inverse, rows, lanes, panel, held)]
        + [tile]
        + [whole(x) for x in (*mine, *other)],
        out_specs=tile,
        scratch_shapes=[
            pltpu.VMEM((PW, PW), BF16),
            pltpu.VMEM((PW, PW), BF16),
            pltpu.VMEM((PB, BS, BS), F32),
            pltpu.VMEM((lc, BS, PW), BF16),
            pltpu.VMEM((lc, BS, PW), BF16),
            pltpu.VMEM((BS, PW), BF16),
            pltpu.VMEM((BS, PW), BF16),
            pltpu.VMEM((BS, PW), F32),
            pltpu.VMEM((512, 256), F32),
            pltpu.VMEM((3, 256, PW), BF16),
        ],
        compiler_params=pltpu.CompilerParams(vmem_limit_bytes=56 << 20),
        cost_estimate=pl.CostEstimate(
            flops=16_000_000_000, bytes_accessed=24 << 20, transcendentals=0
        ),
        name="schur_update",
    )(place, pattern, inverse, rows, lanes, panel, held, e, *mine, *other)


def after(x, *first):
    return lax.optimization_barrier((x,) + first)[0]


def scatter_quarters(quarters, col):
    got = jnp.where(col < PB, quarters[0], 0.0)
    for q in range(1, 4):
        got = got + lax.ppermute(quarters[q], "col", [(k, HOLDER[k][q]) for k in range(PB)])
    return got


def shift_plane(x, dx, dy):
    pairs = []
    for c in range(16):
        at_x, at_y, core = c // 8, (c // 2) % 4, c % 2
        pairs.append((c, ((at_x + dx) % 2) * 8 + ((at_y + dy) % 4) * 2 + core))
    return lax.ppermute(x, "col", pairs)


def gather_corner(piece):
    both = jnp.stack([piece, shift_plane(piece, 1, 0)])
    up, down = shift_plane(both, 0, 1), shift_plane(both, 0, 3)
    return [both, up, down, shift_plane(up[0], 0, 1), shift_plane(down[1], 0, 3)]


def gather_panel(piece):
    both = jnp.stack([piece, shift_plane(piece, 1, 0)])
    return [both] + [shift_plane(both, 0, dy) for dy in (1, 2, 3)]


def swap_cores(pieces):
    return [lax.ppermute(x, "col", [(c, c ^ 1) for c in range(16)]) for x in pieces]


def shift_row(x, d):
    return lax.ppermute(x, "row", [(z, (z + d) % 8) for z in range(8)])


def per_device(front, child_update, child_map, pattern):
    row = lax.axis_index("row")
    col = lax.axis_index("col")
    place = jnp.stack([row, col, col % 2, (col // 2) % 4, col // 8]).astype(jnp.int32)
    blocks = front[0].transpose(0, 2, 1, 3)
    lr, lc = blocks.shape[:2]
    msg, corner_child, part, rows, cols, lanes, panel_sub, panel_lanes = pack(
        place, child_map[0].reshape(16, 128), child_update[0]
    )
    lead = blocks[:, 0].reshape(lr, 4, QUARTER, BS)

    corner = scatter_quarters([lead[0, q] for q in range(4)], col)
    corner = jnp.concatenate([corner, corner_child], axis=0)
    from_far = shift_row(corner, 4)
    low = jnp.where(row < PB, corner, from_far)
    high = jnp.where(row < PB, from_far, corner)
    corner = jnp.concatenate([low, high[QUARTER:]], axis=0)
    corner = jnp.stack([corner, shift_row(corner, 1), shift_row(corner, 2), shift_row(corner, 7)])
    corner_mine = gather_corner(corner)
    corner_other = swap_cores(corner_mine)
    inverse = corner_inverse(place, panel_sub, panel_lanes, corner_mine, corner_other)

    own = scatter_quarters([lead[:, q] for q in range(4)], col)
    sent = own.reshape(lr, 8, 8, BS).transpose(1, 0, 2, 3).reshape(8, lr * 8, BS)
    sent = jnp.concatenate([sent, msg], axis=1)
    sent = lax.all_to_all(sent, "row", split_axis=0, concat_axis=0, tiled=True)
    turned = turn(sent[:, lr * 8:])
    strips = sent[:, :lr * 8].reshape(8, lc, 2, 8, BS).transpose(2, 0, 1, 3, 4)
    sent = jnp.concatenate(
        [strips.reshape(16, lc * 8, BS), turned.reshape(16, 8, BS), part], axis=1
    )
    sent = lax.all_to_all(sent, "col", split_axis=0, concat_axis=0, tiled=True)
    e = extend_add(sent[:, lc * 8:lc * 8 + 8].reshape(128, 256), rows, cols, blocks)
    held = jnp.concatenate(
        [
            sent[:, :lc * 8].reshape(16 * lc * 8, BS),
            sent[:, lc * 8 + 8:].reshape(4, 4, 8, BS).sum(1).reshape(32, BS),
        ],
        axis=0,
    )
    held = lax.all_gather(held, "row", axis=0, tiled=False)

    own = jnp.concatenate([own.reshape(lr * QUARTER, BS), turned[:32]], axis=0)
    panel_mine = gather_panel(own)
    panel_other = swap_cores(panel_mine[:1] + [after(x, inverse) for x in panel_mine[1:]])
    out = schur_update(
        place, pattern[0], inverse, rows, lanes, panel_sub, held, e, panel_mine, panel_other
    )
    return out.transpose(0, 2, 1, 3)[None]


def solution(mesh):
    placed = (
        P("front", None, "row", None, "col"),
        P("front", "row", "col"),
        P("front", None),
        P("front", None, None),
    )
    return jax.shard_map(
        per_device,
        mesh=mesh,
        in_specs=placed,
        out_specs=P("front", None, "row", None, "col"),
        check_vma=False,
    )
```

```python
import functools

import jax
import jax.numpy as jnp
from jax import lax
from jax.experimental import pallas as pl
from jax.experimental.pallas import tpu as pltpu
from jax.sharding import PartitionSpec as P

BS = 256
PB = 4
PW = 1024
KB = 128
F32 = jnp.float32
BF16 = jnp.bfloat16
HIGHEST = lax.Precision.HIGHEST
QUARTER = BS // 4

HOLDER = ((0, 6, 8, 14), (1, 7, 9, 15), (2, 4, 10, 12), (3, 5, 11, 13))
CORNER_SHIFTS = (
    (0, 0, 0, 0), (1, 0, 0, 1), (0, 1, 1, 0), (1, 1, 1, 1),
    (0, 3, 2, 0), (1, 3, 2, 1), (0, 2, 3, None), (1, 2, 4, None),
)
PANEL_SHIFTS = tuple((dx, dy, dy, dx) for dy in range(4) for dx in range(2))


def nn(a, b, precision=None):
    return lax.dot_general(
        a, b, (((1,), (0,)), ((), ())), precision=precision, preferred_element_type=F32
    )


def nt(a, b, precision=None):
    return lax.dot_general(
        a, b, (((1,), (1,)), ((), ())), precision=precision, preferred_element_type=F32
    )


def iota(shape, dim):
    return lax.broadcasted_iota(jnp.int32, shape, dim)


def split2(x):
    high = x.astype(BF16)
    return high, (x - high.astype(F32)).astype(BF16)


def split3(x):
    high = x.astype(BF16)
    rest = x - high.astype(F32)
    middle = rest.astype(BF16)
    return high, middle, (rest - middle.astype(F32)).astype(BF16)


def pack_kernel(
    place, map_ref, update_ref, msg_ref, corner_ref, part_ref,
    rows_ref, cols_ref, lanes_ref, panel_ref, panel_lanes_ref, rank_s, class_s, turned_s,
):
    row, col = place[0], place[1]
    mapping = map_ref[...]
    owner = (mapping >> 8) & 15
    hot = (iota((16, 16, 128), 1) == owner[:, None, :]).astype(F32)
    before = (iota((128, 128), 0) < iota((128, 128), 1)).astype(F32).astype(BF16)
    counts = nn(hot.reshape(256, 128).astype(BF16), before).reshape(16, 16, 128)
    rank = jnp.sum(hot * counts, axis=1).astype(jnp.int32)
    rank_s[...] = rank
    class_s[...] = owner
    slot = owner * 8 + rank
    col_slot = class_s[pl.ds(col, 1), :] * 8 + rank_s[pl.ds(col, 1), :]
    col_hot = (iota((128, 128), 0) == col_slot).astype(F32)
    row_hot = []
    for run in range(2):
        this = class_s[pl.ds(2 * row + run, 1), :]
        row_slot = (this & 7) * 32 + run * 16 + (this >> 3) * 8 + rank_s[pl.ds(2 * row + run, 1), :]
        row_hot.append((iota((256, 128), 0) == row_slot).astype(F32))
    moved = nt(update_ref[...], col_hot, HIGHEST)
    moved = nn(jnp.concatenate(row_hot, axis=1), moved, HIGHEST)
    part_ref[...] = jnp.zeros((16, 8, 256), F32)
    for r in range(8):
        for half in range(2):
            msg_ref[r, :, half * 128:(half + 1) * 128] = moved[
                r * 32 + half * 16:r * 32 + half * 16 + 16, :
            ]
        for run in range(2):
            for upper in range(2):
                at = r * 32 + run * 16 + upper * 8
                piece = moved[at:at + 8, 0:32]
                if upper == 0 and r < PB:
                    g = run * 4 + r
                    corner_ref[:, g * 32:(g + 1) * 32] = piece
                for slot_lane in range(4):

                    @pl.when((col & 3) == slot_lane)
                    def _():
                        lo = run * 128 + slot_lane * 32
                        part_ref[upper * 8 + r, :, lo:lo + 32] = piece

    parts = jnp.concatenate([mapping >> 7, mapping & 127], axis=0).astype(F32).astype(BF16)
    ordered = jnp.zeros((16, 128), F32)
    for run in range(16):
        run_hot = (iota((128, 128), 0) == slot[run:run + 1, :]).astype(F32).astype(BF16)
        moved_map = nt(parts, run_hot)
        both_parts = moved_map[:16] * 128.0 + moved_map[16:]
        ordered = jnp.where(iota((16, 128), 0) == run, both_parts, ordered)
    turned_s[...] = jnp.concatenate([ordered, jnp.zeros((112, 128), F32)], axis=0).T
    mine = turned_s[pl.ds(pl.multiple_of(col * 8, 8), 8), :]
    lead = turned_s[0:32, :]
    for run in range(16):
        cols_ref[run * 8:(run + 1) * 8, :] = jnp.broadcast_to(
            mine[:, run:run + 1], (8, 128)
        ).astype(jnp.int32)
        panel_ref[run * 32:(run + 1) * 32, :] = jnp.broadcast_to(
            lead[:, run:run + 1], (32, 128)
        ).astype(jnp.int32)
    whole = ordered.astype(jnp.int32)
    parts = jnp.concatenate([whole >> 7, whole & 127], axis=0).astype(F32).astype(BF16)

    def spread(ref, width, slot_of, run_of):
        lane = iota((128, width), 1)
        pick = (iota((128, width), 0) == slot_of(lane)).astype(F32).astype(BF16)
        value = nn(parts, pick)
        value = value[:16] * 128.0 + value[16:]
        value = jnp.where(run_of(iota((16, width), 1)) == iota((16, width), 0), value, 0.0)
        ref[...] = jnp.broadcast_to(jnp.sum(value, axis=0, keepdims=True), (8, width)).astype(
            jnp.int32
        )

    spread(rows_ref, 256, lambda n: (((n >> 3) & 1) * 8 + row) * 8 + (n & 7), lambda n: n >> 4)
    spread(lanes_ref, 128, lambda n: col * 8 + (n & 7), lambda n: n >> 3)
    spread(panel_lanes_ref, 512, lambda n: n & 31, lambda n: n >> 5)


def pack(place, mapping, update):
    smem = pl.BlockSpec(memory_space=pltpu.SMEM)
    vmem = pl.BlockSpec(memory_space=pltpu.VMEM)
    ints = lambda *shape: jax.ShapeDtypeStruct(shape, jnp.int32)
    return pl.pallas_call(
        pack_kernel,
        out_shape=(
            jax.ShapeDtypeStruct((8, 16, 256), F32),
            jax.ShapeDtypeStruct((8, 256), F32),
            jax.ShapeDtypeStruct((16, 8, 256), F32),
            ints(8, 256),
            ints(128, 128),
            ints(8, 128),
            ints(512, 128),
            ints(8, 512),
        ),
        in_specs=[smem, vmem, vmem],
        out_specs=(vmem,) * 8,
        scratch_shapes=[
            pltpu.VMEM((16, 128), jnp.int32),
            pltpu.VMEM((16, 128), jnp.int32),
            pltpu.VMEM((128, 128), F32),
        ],
        name="pack",
    )(place, mapping, update)


def turn_kernel(recv_ref, out_ref):
    pieces = []
    for r in range(8):
        pieces += [recv_ref[r, :, 0:128], recv_ref[r, :, 128:256]]
    out_ref[...] = jnp.concatenate(pieces, axis=0).T


def turn(recv):
    vmem = pl.BlockSpec(memory_space=pltpu.VMEM)
    return pl.pallas_call(
        turn_kernel,
        out_shape=jax.ShapeDtypeStruct((128, 256), F32),
        in_specs=[vmem],
        out_specs=vmem,
        name="turn",
    )(recv)


def row_place(g):
    return ((g >> 11) << 8) + (g & 255)


def col_place(g):
    return ((g >> 12) << 8) + (g & 255)


def as_hot(mask):
    return mask.astype(F32).astype(BF16)


def factor_inverse(block):
    a = [block[8 * s:8 * s + 8, :] for s in range(16)]
    sub, lane = iota((8, 128), 0), iota((8, 128), 1)
    lanes_of = lambda x, j: jnp.broadcast_to(x[:, j:j + 1], (8, 128))
    row_of = lambda x, i: jnp.broadcast_to(x[i:i + 1, :], (8, 128))
    for s in range(16):
        js = [8 * s + q for q in range(8)]
        c = [lanes_of(a[s], j) for j in js]
        strip = a[s]
        rows, mult = [], [[None] * 8 for _ in range(8)]
        pivots = jnp.zeros((8, 128), F32)
        for q in range(8):
            pivot = row_of(c[q], q)
            over = 1.0 / pivot
            pivots = jnp.where(sub == q, pivot, pivots)
            below = jnp.where(sub > q, c[q], 0.0)
            strip = jnp.where(lane == js[q], jnp.where(sub == q, 1.0, 0.0), strip)
            row = row_of(strip, q) * over
            rows.append(jnp.where((lane <= js[q]) | (lane > js[7]), row, 0.0))
            for q2 in range(q + 1, 8):
                m = row_of(c[q2], q) * over
                mult[q][q2] = m
                c[q2] = c[q2] - below * m
            strip = strip - below * row
        a[s] = jnp.where(lane <= sub + 8 * s, strip, 0.0) * lax.rsqrt(pivots)
        kept = (lane < js[0]) | (lane > js[7])
        for t in range(s + 1, 16):
            ct = [lanes_of(a[t], j) for j in js]
            for q in range(8):
                for q2 in range(q + 1, 8):
                    ct[q2] = ct[q2] - ct[q] * mult[q][q2]
            value = jnp.where(kept, a[t], 0.0)
            for q in range(8):
                value = value - ct[q] * rows[q]
            a[t] = value
    return jnp.concatenate(a, axis=0)


def holders(place, mine, other, shifts):
    core, y, x = place[2], place[3], place[4]
    for refs, at_core in ((mine, core), (other, 1 - core)):
        for dx, dy, index, part in shifts:
            ref = refs[index] if part is None else refs[index].at[part]
            from_x, from_y = (x - dx) & 1, (y - dy) & 3
            middle = ((from_y + 1) >> 1) & 1
            yield ref, from_x * 8 + from_y * 2 + at_core, at_core + 2 * middle, from_x * 2 + (from_y >> 1)


def corner_kernel(place, panel_ref, lanes_ref, *refs):
    mine, other = refs[:5], refs[5:10]
    inv_ref, s_ref, raw_s, child_s, placed_s = refs[10:]
    n, b = PW // KB, KB
    row = place[0]
    slot_of = iota((8, 128), 1) >> 5
    for ref, holder, k, q in holders(place, mine, other, CORNER_SHIFTS):
        for block in range(PB):
            start = pl.multiple_of(block * BS + q * QUARTER, QUARTER)
            raw_s[k, pl.ds(start, QUARTER), :] = ref[(row - block) & 3, 0:QUARTER, :]
        lane_slot = holder & 3
        for block in range(2 * PB):
            at = QUARTER + (block // PB) * 8
            for half in range(2):
                value = ref[(row - block) & 3, at:at + 8, half * 128:(half + 1) * 128]
                for g in range(4):
                    start = (block * 2 + half) * 32 + g * 8
                    shifted = pltpu.roll(value, ((lane_slot - g) & 3) * 32, 1)
                    old = child_s[holder >> 2, start:start + 8, :]
                    child_s[holder >> 2, start:start + 8, :] = jnp.where(
                        slot_of == lane_slot, shifted, old
                    )
    child = jnp.concatenate([child_s[i] for i in range(4)], axis=1)
    child = 0.5 * (child + child.T)
    col_hot = as_hot(panel_ref[:, 0:1] == iota((512, PW), 1))
    placed_s[...] = sum(nn(part, col_hot) for part in split3(child))
    lanes = lanes_ref[0:1, :]
    raw = lambda i, j: raw_s[j // 2, i * b:(i + 1) * b, (j % 2) * b:(j % 2 + 1) * b]
    for i in range(n):
        row_hot = as_hot(iota((b, 512), 0) + i * b == lanes)
        added = sum(nn(row_hot, part) for part in split3(placed_s[:, :(i + 1) * b]))
        for j in range(i + 1):
            s_ref[i * b:(i + 1) * b, j * b:(j + 1) * b] = (
                0.5 * (raw(i, j) + raw(j, i).T) + added[:, j * b:(j + 1) * b]
            )
    for k in range(n):
        lo, hi = k * b, (k + 1) * b
        diag = factor_inverse(s_ref[lo:hi, lo:hi])
        if k < n - 1:
            below = nt(s_ref[hi:, lo:hi], diag, HIGHEST)
            s_ref[hi:, hi:hi + b] = s_ref[hi:, hi:hi + b] - nt(below, below[:b], HIGHEST)
        if k > 0:
            left = nn(diag, inv_ref[lo:hi, :lo], HIGHEST)
            inv_ref[lo:hi, :lo] = left
        inv_ref[lo:hi, lo:hi] = diag
        if k < n - 1:
            inv_ref[lo:hi, hi:] = jnp.zeros((b, PW - hi), F32)
            for j in range(k + 2, n):
                at = (j - k - 1) * b
                s_ref[j * b:, j * b:(j + 1) * b] = s_ref[j * b:, j * b:(j + 1) * b] - nt(
                    below[at:], below[at:at + b], HIGHEST
                )
            if k > 0:
                inv_ref[hi:, :lo] = inv_ref[hi:, :lo] - nn(below, left, HIGHEST)
            inv_ref[hi:, lo:hi] = -nn(below, diag, HIGHEST)


def corner_inverse(place, panel, lanes, mine, other):
    smem = pl.BlockSpec(memory_space=pltpu.SMEM)
    vmem = pl.BlockSpec(memory_space=pltpu.VMEM)
    return pl.pallas_call(
        corner_kernel,
        out_shape=jax.ShapeDtypeStruct((PW, PW), F32),
        in_specs=[smem] + [vmem] * 12,
        out_specs=vmem,
        scratch_shapes=[
            pltpu.VMEM((PW, PW), F32),
            pltpu.VMEM((PB, PW, BS), F32),
            pltpu.VMEM((4, 512, 128), F32),
            pltpu.VMEM((512, PW), F32),
        ],
        compiler_params=pltpu.CompilerParams(vmem_limit_bytes=48 << 20),
        cost_estimate=pl.CostEstimate(
            flops=40_000_000_000, bytes_accessed=8 << 20, transcendentals=0
        ),
        name="corner_inverse",
    )(place, panel, lanes, *mine, *other)


def three_pass(a, b):
    return nt(a[0], b[0]) + nt(a[0], b[1]) + nt(a[1], b[0])


def schur_kernel(
    place, pattern, inv_ref, rows_ref, cols_ref, lanes_ref, panel_ref, landed_ref, held_ref, front_ref, *refs
):
    mine, other = refs[:4], refs[4:8]
    (out_ref, inv_h, inv_l, raw_s, col_h, col_l, row_h, row_l, row_f, child_s, child_p) = refs[8:]
    row, col = place[0], place[1]
    step = pl.program_id(0)
    per, lc = out_ref.shape[:2]

    def solve(raw, high_ref, low_ref, full_ref=None):
        raw = split2(raw)
        for j in range(PB):
            lo, deep = j * BS, (j + 1) * BS
            value = three_pass(
                (raw[0][:, :deep], raw[1][:, :deep]), (inv_h[lo:deep, :deep], inv_l[lo:deep, :deep])
            )
            high_ref[:, lo:deep], low_ref[:, lo:deep] = split2(value)
            if full_ref is not None:
                full_ref[:, lo:deep] = value

    @pl.when(step == 0)
    def _():
        for j in range(PB):
            high, low = split2(inv_ref[j * BS:(j + 1) * BS, :])
            inv_h[j * BS:(j + 1) * BS, :] = high
            inv_l[j * BS:(j + 1) * BS, :] = low
        col_hot = as_hot(panel_ref[:, 0:1] == iota((512, PW), 1))
        held_child = []
        for run in range(16):
            held_child.append(
                jnp.concatenate(
                    [
                        held_ref[run // 2, 384 + g * 8:392 + g * 8, (run % 2) * 128:(run % 2 + 1) * 128]
                        for g in range(4)
                    ],
                    axis=1,
                )
            )
        held_child = jnp.concatenate(held_child, axis=0)
        placed = split2(sum(nn(part, col_hot) for part in split2(held_child)))
        raw = []
        for k in range(PB):
            column = []
            for m in range(lc):
                for q in range(4):
                    at = HOLDER[k][q] * 24 + m * 8
                    column += [held_ref[r, at:at + 8, :] for r in range(8)]
            raw.append(jnp.concatenate(column, axis=0))
        raw = jnp.concatenate(raw, axis=1)
        row_hot = as_hot(iota((lc * BS, 128), 0) == col_place(lanes_ref[0:1, :]))
        solve(raw + sum(nn(row_hot, part) for part in placed), col_h, col_l)
        for ref, holder, k, q in holders(place, mine, other, PANEL_SHIFTS):
            child_s[pl.ds(pl.multiple_of(holder * 32, 32), 32), :] = ref[384:416, :]
        placed = sum(nn(part, col_hot) for part in split2(child_s[...].T))
        child_p[0], child_p[1] = split2(placed)

    for ref, holder, k, q in holders(place, mine, other, PANEL_SHIFTS):
        for h in range(per):
            start = pl.multiple_of(h * BS + q * QUARTER, QUARTER)
            at = pl.multiple_of((step * per + h) * QUARTER, QUARTER)
            raw_s[k, pl.ds(start, QUARTER), :] = ref[pl.ds(at, QUARTER), :]
    row_hot = as_hot(
        iota((per * BS, 256), 0) + step * (per * BS) == row_place(rows_ref[0:1, :])
    )
    raw_rows = jnp.concatenate([raw_s[k] for k in range(PB)], axis=1)
    raw_rows = raw_rows + nn(row_hot, child_p[0]) + nn(row_hot, child_p[1])
    solve(raw_rows, row_h, row_l, row_f)

    added = split3(sum(nt(row_hot, part) for part in split3(landed_ref[...])))
    for m in range(lc):
        col_hot = as_hot(col_place(cols_ref[:, 0:1]) == iota((128, BS), 1) + m * BS)
        e = sum(nn(part, col_hot) for part in added)
        block_col = m * 16 + col
        for h in range(per):
            block_row = (step * per + h) * 8 + row
            at = slice(h * BS, (h + 1) * BS)
            out_ref[h, m] = front_ref[h, m] + e[at]
            applied = (pattern[block_row, block_col] == 1) & (block_row >= PB) & (block_col >= PB)

            @pl.when(applied)
            def _():
                out_ref[h, m] = out_ref[h, m] - three_pass(
                    (row_h[at], row_l[at]),
                    (col_h[m * BS:(m + 1) * BS], col_l[m * BS:(m + 1) * BS]),
                )

    @pl.when(col < PB)
    def _():
        start = pl.multiple_of(jnp.minimum(col, PB - 1) * BS, BS)
        for h in range(per):
            out_ref[h, 0] = row_f[h * BS:(h + 1) * BS, pl.ds(start, BS)]


def schur_update(place, pattern, inverse, rows, cols, lanes, panel, landed, held, blocks, mine, other):
    lr, lc = blocks.shape[:2]
    per = 2
    smem = pl.BlockSpec(memory_space=pltpu.SMEM)
    whole = lambda x: pl.BlockSpec(x.shape, lambda l: (0,) * x.ndim)
    tile = pl.BlockSpec((per, lc, BS, BS), lambda l: (l, 0, 0, 0))
    return pl.pallas_call(
        schur_kernel,
        grid=(lr // per,),
        out_shape=jax.ShapeDtypeStruct(blocks.shape, F32),
        in_specs=[smem, smem]
        + [whole(x) for x in (inverse, rows, cols, lanes, panel, landed, held)]
        + [tile]
        + [whole(x) for x in (*mine, *other)],
        out_specs=tile,
        scratch_shapes=[
            pltpu.VMEM((PW, PW), BF16),
            pltpu.VMEM((PW, PW), BF16),
            pltpu.VMEM((PB, per * BS, BS), F32),
            pltpu.VMEM((lc * BS, PW), BF16),
            pltpu.VMEM((lc * BS, PW), BF16),
            pltpu.VMEM((per * BS, PW), BF16),
            pltpu.VMEM((per * BS, PW), BF16),
            pltpu.VMEM((per * BS, PW), F32),
            pltpu.VMEM((512, 256), F32),
            pltpu.VMEM((2, 256, PW), BF16),
        ],
        compiler_params=pltpu.CompilerParams(vmem_limit_bytes=60 << 20),
        cost_estimate=pl.CostEstimate(
            flops=16_000_000_000, bytes_accessed=24 << 20, transcendentals=0
        ),
        name="schur_update",
    )(place, pattern, inverse, rows, cols, lanes, panel, landed, held, blocks, *mine, *other)


def after(x, *first):
    return lax.optimization_barrier((x,) + first)[0]


def scatter_quarters(quarters, col):
    got = jnp.where(col < PB, quarters[0], 0.0)
    for q in range(1, 4):
        got = got + lax.ppermute(quarters[q], "col", [(k, HOLDER[k][q]) for k in range(PB)])
    return got


def shift_plane(x, dx, dy):
    pairs = []
    for c in range(16):
        at_x, at_y, core = c // 8, (c // 2) % 4, c % 2
        pairs.append((c, ((at_x + dx) % 2) * 8 + ((at_y + dy) % 4) * 2 + core))
    return lax.ppermute(x, "col", pairs)


def gather_corner(piece):
    both = jnp.stack([piece, shift_plane(piece, 1, 0)])
    up, down = shift_plane(both, 0, 1), shift_plane(both, 0, 3)
    return [both, up, down, shift_plane(up[0], 0, 1), shift_plane(down[1], 0, 3)]


def gather_panel(piece):
    both = jnp.stack([piece, shift_plane(piece, 1, 0)])
    return [both] + [shift_plane(both, 0, dy) for dy in (1, 2, 3)]


def swap_cores(pieces):
    return [lax.ppermute(x, "col", [(c, c ^ 1) for c in range(16)]) for x in pieces]


def shift_row(x, d):
    return lax.ppermute(x, "row", [(z, (z + d) % 8) for z in range(8)])


def per_device(front, child_update, child_map, pattern):
    row = lax.axis_index("row")
    col = lax.axis_index("col")
    place = jnp.stack([row, col, col % 2, (col // 2) % 4, col // 8]).astype(jnp.int32)
    blocks = front[0].transpose(0, 2, 1, 3)
    lr, lc = blocks.shape[:2]
    msg, corner_child, part, rows, cols, lanes, panel_sub, panel_lanes = pack(
        place, child_map[0].reshape(16, 128), child_update[0]
    )

    first = blocks[0, 0]
    first = scatter_quarters([first[q * QUARTER:(q + 1) * QUARTER] for q in range(4)], col)
    corner = jnp.concatenate([first, corner_child], axis=0)
    from_far = shift_row(corner, 4)
    low = jnp.where(row < PB, corner, from_far)
    high = jnp.where(row < PB, from_far, corner)
    corner = jnp.concatenate([low, high[QUARTER:]], axis=0)
    corner = jnp.stack([corner, shift_row(corner, 1), shift_row(corner, 2), shift_row(corner, 7)])
    corner_mine = gather_corner(corner)
    over_planes = corner
    corner_other = swap_cores(corner_mine)
    inverse = corner_inverse(place, panel_sub, panel_lanes, corner_mine, corner_other)

    lead = after(blocks[:, 0], first).reshape(lr, 4, QUARTER, BS)
    own = scatter_quarters([lead[:, q] for q in range(4)], col)
    sent = own.reshape(lr, 8, 8, BS).transpose(1, 0, 2, 3).reshape(8, lr * 8, BS)
    sent = after(jnp.concatenate([sent, msg], axis=1), over_planes)
    sent = lax.all_to_all(sent, "row", split_axis=0, concat_axis=0, tiled=True)
    turned = turn(sent[:, lr * 8:])
    strips = sent[:, :lr * 8].reshape(8, lc, 2, 8, BS).transpose(2, 0, 1, 3, 4)
    sent = jnp.concatenate(
        [strips.reshape(16, lc * 8, BS), turned.reshape(16, 8, BS), part], axis=1
    )
    sent = lax.all_to_all(sent, "col", split_axis=0, concat_axis=0, tiled=True)
    landed = sent[:, lc * 8:lc * 8 + 8].reshape(128, 256)
    held = jnp.concatenate(
        [
            sent[:, :lc * 8].reshape(16 * lc * 8, BS),
            sent[:, lc * 8 + 8:].reshape(4, 4, 8, BS).sum(1).reshape(32, BS),
        ],
        axis=0,
    )
    held = lax.all_gather(held, "row", axis=0, tiled=False)

    own = jnp.concatenate([own.reshape(lr * QUARTER, BS), turned[:32]], axis=0)
    panel_mine = gather_panel(own)
    panel_other = swap_cores(panel_mine[:1] + [after(x, inverse) for x in panel_mine[1:]])
    out = schur_update(
        place, pattern[0], inverse, rows, cols, lanes, panel_sub, landed, held, blocks,
        panel_mine, panel_other,
    )
    return out.transpose(0, 2, 1, 3)[None]


def solution(mesh):
    placed = (
        P("front", None, "row", None, "col"),
        P("front", "row", "col"),
        P("front", None),
        P("front", None, None),
    )
    return jax.shard_map(
        per_device,
        mesh=mesh,
        in_specs=placed,
        out_specs=P("front", None, "row", None, "col"),
        check_vma=False,
    )
```

```python
import functools

import jax
import jax.numpy as jnp
from jax import lax
from jax.experimental import pallas as pl
from jax.experimental.pallas import tpu as pltpu
from jax.sharding import PartitionSpec as P

BS = 256
PB = 4
PW = 1024
KB = 128
F32 = jnp.float32
BF16 = jnp.bfloat16
HIGHEST = lax.Precision.HIGHEST
QUARTER = BS // 4

HOLDER = ((0, 6, 8, 14), (1, 7, 9, 15), (2, 4, 10, 12), (3, 5, 11, 13))
CORNER_SHIFTS = (
    (0, 0, 0, 0), (1, 0, 0, 1), (0, 1, 1, 0), (1, 1, 1, 1),
    (0, 3, 2, 0), (1, 3, 2, 1), (0, 2, 3, None), (1, 2, 4, None),
)
PANEL_SHIFTS = tuple((dx, dy, dy, dx) for dy in range(4) for dx in range(2))


def nn(a, b, precision=None):
    return lax.dot_general(
        a, b, (((1,), (0,)), ((), ())), precision=precision, preferred_element_type=F32
    )


def nt(a, b, precision=None):
    return lax.dot_general(
        a, b, (((1,), (1,)), ((), ())), precision=precision, preferred_element_type=F32
    )


def iota(shape, dim):
    return lax.broadcasted_iota(jnp.int32, shape, dim)


def split2(x):
    high = x.astype(BF16)
    return high, (x - high.astype(F32)).astype(BF16)


def split3(x):
    high = x.astype(BF16)
    rest = x - high.astype(F32)
    middle = rest.astype(BF16)
    return high, middle, (rest - middle.astype(F32)).astype(BF16)


def pack_kernel(
    place, map_ref, update_ref, msg_ref, corner_ref, part_ref,
    rows_ref, cols_ref, lanes_ref, panel_ref, panel_lanes_ref, rank_s, class_s, turned_s,
):
    row, col = place[0], place[1]
    mapping = map_ref[...]
    owner = (mapping >> 8) & 15
    hot = (iota((16, 16, 128), 1) == owner[:, None, :]).astype(F32)
    before = (iota((128, 128), 0) < iota((128, 128), 1)).astype(F32).astype(BF16)
    counts = nn(hot.reshape(256, 128).astype(BF16), before).reshape(16, 16, 128)
    rank = jnp.sum(hot * counts, axis=1).astype(jnp.int32)
    rank_s[...] = rank
    class_s[...] = owner
    slot = owner * 8 + rank
    col_slot = class_s[pl.ds(col, 1), :] * 8 + rank_s[pl.ds(col, 1), :]
    col_hot = (iota((128, 128), 0) == col_slot).astype(F32)
    row_hot = []
    for run in range(2):
        this = class_s[pl.ds(2 * row + run, 1), :]
        row_slot = (this & 7) * 32 + run * 16 + (this >> 3) * 8 + rank_s[pl.ds(2 * row + run, 1), :]
        row_hot.append((iota((256, 128), 0) == row_slot).astype(F32))
    moved = nt(update_ref[...], col_hot, HIGHEST)
    moved = nn(jnp.concatenate(row_hot, axis=1), moved, HIGHEST)
    part_ref[...] = jnp.zeros((16, 8, 256), F32)
    for r in range(8):
        for half in range(2):
            msg_ref[r, :, half * 128:(half + 1) * 128] = moved[
                r * 32 + half * 16:r * 32 + half * 16 + 16, :
            ]
        for run in range(2):
            for upper in range(2):
                at = r * 32 + run * 16 + upper * 8
                piece = moved[at:at + 8, 0:32]
                if upper == 0 and r < PB:
                    g = run * 4 + r
                    corner_ref[:, g * 32:(g + 1) * 32] = piece
                for slot_lane in range(4):

                    @pl.when((col & 3) == slot_lane)
                    def _():
                        lo = run * 128 + slot_lane * 32
                        part_ref[upper * 8 + r, :, lo:lo + 32] = piece

    parts = jnp.concatenate([mapping >> 7, mapping & 127], axis=0).astype(F32).astype(BF16)
    ordered = jnp.zeros((16, 128), F32)
    for run in range(16):
        run_hot = (iota((128, 128), 0) == slot[run:run + 1, :]).astype(F32).astype(BF16)
        moved_map = nt(parts, run_hot)
        both_parts = moved_map[:16] * 128.0 + moved_map[16:]
        ordered = jnp.where(iota((16, 128), 0) == run, both_parts, ordered)
    turned_s[...] = jnp.concatenate([ordered, jnp.zeros((112, 128), F32)], axis=0).T
    mine = turned_s[pl.ds(pl.multiple_of(col * 8, 8), 8), :]
    lead = turned_s[0:32, :]
    for run in range(16):
        cols_ref[run * 8:(run + 1) * 8, :] = jnp.broadcast_to(
            mine[:, run:run + 1], (8, 128)
        ).astype(jnp.int32)
        panel_ref[run * 32:(run + 1) * 32, :] = jnp.broadcast_to(
            lead[:, run:run + 1], (32, 128)
        ).astype(jnp.int32)
    whole = ordered.astype(jnp.int32)
    parts = jnp.concatenate([whole >> 7, whole & 127], axis=0).astype(F32).astype(BF16)

    def spread(ref, width, slot_of, run_of):
        lane = iota((128, width), 1)
        pick = (iota((128, width), 0) == slot_of(lane)).astype(F32).astype(BF16)
        value = nn(parts, pick)
        value = value[:16] * 128.0 + value[16:]
        value = jnp.where(run_of(iota((16, width), 1)) == iota((16, width), 0), value, 0.0)
        ref[...] = jnp.broadcast_to(jnp.sum(value, axis=0, keepdims=True), (8, width)).astype(
            jnp.int32
        )

    spread(rows_ref, 256, lambda n: (((n >> 3) & 1) * 8 + row) * 8 + (n & 7), lambda n: n >> 4)
    spread(lanes_ref, 128, lambda n: col * 8 + (n & 7), lambda n: n >> 3)
    spread(panel_lanes_ref, 512, lambda n: n & 31, lambda n: n >> 5)


def pack(place, mapping, update):
    smem = pl.BlockSpec(memory_space=pltpu.SMEM)
    vmem = pl.BlockSpec(memory_space=pltpu.VMEM)
    ints = lambda *shape: jax.ShapeDtypeStruct(shape, jnp.int32)
    return pl.pallas_call(
        pack_kernel,
        out_shape=(
            jax.ShapeDtypeStruct((8, 16, 256), F32),
            jax.ShapeDtypeStruct((8, 256), F32),
            jax.ShapeDtypeStruct((16, 8, 256), F32),
            ints(8, 256),
            ints(128, 128),
            ints(8, 128),
            ints(512, 128),
            ints(8, 512),
        ),
        in_specs=[smem, vmem, vmem],
        out_specs=(vmem,) * 8,
        scratch_shapes=[
            pltpu.VMEM((16, 128), jnp.int32),
            pltpu.VMEM((16, 128), jnp.int32),
            pltpu.VMEM((128, 128), F32),
        ],
        name="pack",
    )(place, mapping, update)


def turn_kernel(recv_ref, out_ref):
    pieces = []
    for r in range(8):
        pieces += [recv_ref[r, :, 0:128], recv_ref[r, :, 128:256]]
    out_ref[...] = jnp.concatenate(pieces, axis=0).T


def turn(recv):
    vmem = pl.BlockSpec(memory_space=pltpu.VMEM)
    return pl.pallas_call(
        turn_kernel,
        out_shape=jax.ShapeDtypeStruct((128, 256), F32),
        in_specs=[vmem],
        out_specs=vmem,
        name="turn",
    )(recv)


def row_place(g):
    return ((g >> 11) << 8) + (g & 255)


def col_place(g):
    return ((g >> 12) << 8) + (g & 255)


def as_hot(mask):
    return mask.astype(F32).astype(BF16)


def factor_inverse(block):
    a = [block[8 * s:8 * s + 8, :] for s in range(16)]
    sub, lane = iota((8, 128), 0), iota((8, 128), 1)
    lanes_of = lambda x, j: jnp.broadcast_to(x[:, j:j + 1], (8, 128))
    row_of = lambda x, i: jnp.broadcast_to(x[i:i + 1, :], (8, 128))
    for s in range(16):
        js = [8 * s + q for q in range(8)]
        c = [lanes_of(a[s], j) for j in js]
        strip = a[s]
        rows, mult = [], [[None] * 8 for _ in range(8)]
        pivots = jnp.zeros((8, 128), F32)
        for q in range(8):
            pivot = row_of(c[q], q)
            over = 1.0 / pivot
            pivots = jnp.where(sub == q, pivot, pivots)
            below = jnp.where(sub > q, c[q], 0.0)
            strip = jnp.where(lane == js[q], jnp.where(sub == q, 1.0, 0.0), strip)
            row = row_of(strip, q) * over
            rows.append(jnp.where((lane <= js[q]) | (lane > js[7]), row, 0.0))
            for q2 in range(q + 1, 8):
                m = row_of(c[q2], q) * over
                mult[q][q2] = m
                c[q2] = c[q2] - below * m
            strip = strip - below * row
        a[s] = jnp.where(lane <= sub + 8 * s, strip, 0.0) * lax.rsqrt(pivots)
        kept = (lane < js[0]) | (lane > js[7])
        for t in range(s + 1, 16):
            ct = [lanes_of(a[t], j) for j in js]
            for q in range(8):
                for q2 in range(q + 1, 8):
                    ct[q2] = ct[q2] - ct[q] * mult[q][q2]
            value = jnp.where(kept, a[t], 0.0)
            for q in range(8):
                value = value - ct[q] * rows[q]
            a[t] = value
    return jnp.concatenate(a, axis=0)


def holders(place, mine, other, shifts):
    core, y, x = place[2], place[3], place[4]
    for refs, at_core in ((mine, core), (other, 1 - core)):
        for dx, dy, index, part in shifts:
            ref = refs[index] if part is None else refs[index].at[part]
            from_x, from_y = (x - dx) & 1, (y - dy) & 3
            middle = ((from_y + 1) >> 1) & 1
            yield ref, from_x * 8 + from_y * 2 + at_core, at_core + 2 * middle, from_x * 2 + (from_y >> 1)


def corner_kernel(place, panel_ref, lanes_ref, *refs):
    mine, other = refs[:5], refs[5:10]
    high_ref, low_ref, inv_ref, s_ref, raw_s, child_s, placed_s = refs[10:]
    n, b = PW // KB, KB
    row = place[0]
    slot_of = iota((8, 128), 1) >> 5
    for ref, holder, k, q in holders(place, mine, other, CORNER_SHIFTS):
        for block in range(PB):
            start = pl.multiple_of(block * BS + q * QUARTER, QUARTER)
            raw_s[k, pl.ds(start, QUARTER), :] = ref[(row - block) & 3, 0:QUARTER, :]
        lane_slot = holder & 3
        for block in range(2 * PB):
            at = QUARTER + (block // PB) * 8
            for half in range(2):
                value = ref[(row - block) & 3, at:at + 8, half * 128:(half + 1) * 128]
                for g in range(4):
                    start = (block * 2 + half) * 32 + g * 8
                    shifted = pltpu.roll(value, ((lane_slot - g) & 3) * 32, 1)
                    old = child_s[holder >> 2, start:start + 8, :]
                    child_s[holder >> 2, start:start + 8, :] = jnp.where(
                        slot_of == lane_slot, shifted, old
                    )
    child = jnp.concatenate([child_s[i] for i in range(4)], axis=1)
    child = 0.5 * (child + child.T)
    col_hot = as_hot(panel_ref[:, 0:1] == iota((512, PW), 1))
    placed_s[...] = sum(nn(part, col_hot) for part in split3(child))
    lanes = lanes_ref[0:1, :]
    raw = lambda i, j: raw_s[j // 2, i * b:(i + 1) * b, (j % 2) * b:(j % 2 + 1) * b]
    for i in range(n):
        row_hot = as_hot(iota((b, 512), 0) + i * b == lanes)
        added = sum(nn(row_hot, part) for part in split3(placed_s[:, :(i + 1) * b]))
        for j in range(i + 1):
            s_ref[i * b:(i + 1) * b, j * b:(j + 1) * b] = (
                0.5 * (raw(i, j) + raw(j, i).T) + added[:, j * b:(j + 1) * b]
            )
    for k in range(n):
        lo, hi = k * b, (k + 1) * b
        diag = factor_inverse(s_ref[lo:hi, lo:hi])
        if k < n - 1:
            below = nt(s_ref[hi:, lo:hi], diag, HIGHEST)
            s_ref[hi:, hi:hi + b] = s_ref[hi:, hi:hi + b] - nt(below, below[:b], HIGHEST)
        if k > 0:
            left = nn(diag, inv_ref[lo:hi, :lo], HIGHEST)
            inv_ref[lo:hi, :lo] = left
        inv_ref[lo:hi, lo:hi] = diag
        high_ref[lo:hi, :hi], low_ref[lo:hi, :hi] = split2(inv_ref[lo:hi, :hi])
        if k % 2 == 0:
            high_ref[lo:hi, hi:hi + b] = jnp.zeros((b, b), BF16)
            low_ref[lo:hi, hi:hi + b] = jnp.zeros((b, b), BF16)
        if k < n - 1:
            for j in range(k + 2, n):
                at = (j - k - 1) * b
                s_ref[j * b:, j * b:(j + 1) * b] = s_ref[j * b:, j * b:(j + 1) * b] - nt(
                    below[at:], below[at:at + b], HIGHEST
                )
            if k > 0:
                inv_ref[hi:, :lo] = inv_ref[hi:, :lo] - nn(below, left, HIGHEST)
            inv_ref[hi:, lo:hi] = -nn(below, diag, HIGHEST)


def corner_inverse(place, panel, lanes, mine, other):
    smem = pl.BlockSpec(memory_space=pltpu.SMEM)
    vmem = pl.BlockSpec(memory_space=pltpu.VMEM)
    return pl.pallas_call(
        corner_kernel,
        out_shape=(jax.ShapeDtypeStruct((PW, PW), BF16),) * 2,
        in_specs=[smem] + [vmem] * 12,
        out_specs=(vmem, vmem),
        scratch_shapes=[
            pltpu.VMEM((PW, PW), F32),
            pltpu.VMEM((PW, PW), F32),
            pltpu.VMEM((PB, PW, BS), F32),
            pltpu.VMEM((4, 512, 128), F32),
            pltpu.VMEM((512, PW), F32),
        ],
        compiler_params=pltpu.CompilerParams(vmem_limit_bytes=48 << 20),
        cost_estimate=pl.CostEstimate(
            flops=40_000_000_000, bytes_accessed=8 << 20, transcendentals=0
        ),
        name="corner_inverse",
    )(place, panel, lanes, *mine, *other)


def three_pass(a, b):
    return nt(a[0], b[0]) + nt(a[0], b[1]) + nt(a[1], b[0])


def solve(raw, inv_h, inv_l, high_ref, low_ref, full_ref=None):
    raw = split2(raw)
    for j in range(PB):
        lo, deep = j * BS, (j + 1) * BS
        value = three_pass(
            (raw[0][:, :deep], raw[1][:, :deep]), (inv_h[lo:deep, :deep], inv_l[lo:deep, :deep])
        )
        high_ref[:, lo:deep], low_ref[:, lo:deep] = split2(value)
        if full_ref is not None:
            full_ref[:, lo:deep] = value


def columns_kernel(inv_h, inv_l, lanes_ref, panel_ref, held_ref, col_h, col_l):
    lc = col_h.shape[0] // BS
    col_hot = as_hot(panel_ref[:, 0:1] == iota((512, PW), 1))
    held_child = []
    for run in range(16):
        held_child.append(
            jnp.concatenate(
                [
                    held_ref[run // 2, 384 + g * 8:392 + g * 8, (run % 2) * 128:(run % 2 + 1) * 128]
                    for g in range(4)
                ],
                axis=1,
            )
        )
    held_child = jnp.concatenate(held_child, axis=0)
    placed = split2(sum(nn(part, col_hot) for part in split2(held_child)))
    raw = []
    for k in range(PB):
        column = []
        for m in range(lc):
            for q in range(4):
                at = HOLDER[k][q] * 24 + m * 8
                column += [held_ref[r, at:at + 8, :] for r in range(8)]
        raw.append(jnp.concatenate(column, axis=0))
    raw = jnp.concatenate(raw, axis=1)
    row_hot = as_hot(iota((lc * BS, 128), 0) == col_place(lanes_ref[0:1, :]))
    solve(raw + sum(nn(row_hot, part) for part in placed), inv_h, inv_l, col_h, col_l)


def solved_columns(inverse, lanes, panel, held, lc):
    vmem = pl.BlockSpec(memory_space=pltpu.VMEM)
    return pl.pallas_call(
        columns_kernel,
        out_shape=(jax.ShapeDtypeStruct((lc * BS, PW), BF16),) * 2,
        in_specs=[vmem] * 5,
        out_specs=(vmem, vmem),
        compiler_params=pltpu.CompilerParams(vmem_limit_bytes=40 << 20),
        cost_estimate=pl.CostEstimate(
            flops=6_000_000_000, bytes_accessed=12 << 20, transcendentals=0
        ),
        name="solved_columns",
    )(*inverse, lanes, panel, held)


def schur_kernel(
    place, pattern, inv_h, inv_l, rows_ref, cols_ref, panel_ref, landed_ref, col_h, col_l, front_ref, *refs
):
    mine, other = refs[:4], refs[4:8]
    out_ref, raw_s, row_h, row_l, row_f, child_s, child_p = refs[8:]
    row, col = place[0], place[1]
    step = pl.program_id(0)
    per, lc = out_ref.shape[:2]

    @pl.when(step == 0)
    def _():
        col_hot = as_hot(panel_ref[:, 0:1] == iota((512, PW), 1))
        for ref, holder, k, q in holders(place, mine, other, PANEL_SHIFTS):
            child_s[pl.ds(pl.multiple_of(holder * 32, 32), 32), :] = ref[384:416, :]
        placed = sum(nn(part, col_hot) for part in split2(child_s[...].T))
        child_p[0], child_p[1] = split2(placed)

    for ref, holder, k, q in holders(place, mine, other, PANEL_SHIFTS):
        for h in range(per):
            start = pl.multiple_of(h * BS + q * QUARTER, QUARTER)
            at = pl.multiple_of((step * per + h) * QUARTER, QUARTER)
            raw_s[k, pl.ds(start, QUARTER), :] = ref[pl.ds(at, QUARTER), :]
    row_hot = as_hot(
        iota((per * BS, 256), 0) + step * (per * BS) == row_place(rows_ref[0:1, :])
    )
    raw_rows = jnp.concatenate([raw_s[k] for k in range(PB)], axis=1)
    raw_rows = raw_rows + nn(row_hot, child_p[0]) + nn(row_hot, child_p[1])
    solve(raw_rows, inv_h, inv_l, row_h, row_l, row_f)

    added = split3(sum(nt(row_hot, part) for part in split3(landed_ref[...])))
    for m in range(lc):
        col_hot = as_hot(col_place(cols_ref[:, 0:1]) == iota((128, BS), 1) + m * BS)
        e = sum(nn(part, col_hot) for part in added)
        block_col = m * 16 + col
        for h in range(per):
            block_row = (step * per + h) * 8 + row
            at = slice(h * BS, (h + 1) * BS)
            out_ref[h, m] = front_ref[h, m] + e[at]
            applied = (pattern[block_row, block_col] == 1) & (block_row >= PB) & (block_col >= PB)

            @pl.when(applied)
            def _():
                out_ref[h, m] = out_ref[h, m] - three_pass(
                    (row_h[at], row_l[at]),
                    (col_h[m * BS:(m + 1) * BS], col_l[m * BS:(m + 1) * BS]),
                )

    @pl.when(col < PB)
    def _():
        start = pl.multiple_of(jnp.minimum(col, PB - 1) * BS, BS)
        for h in range(per):
            out_ref[h, 0] = row_f[h * BS:(h + 1) * BS, pl.ds(start, BS)]


def schur_update(place, pattern, inverse, rows, cols, panel, landed, solved, blocks, mine, other):
    lr, lc = blocks.shape[:2]
    per = 2
    smem = pl.BlockSpec(memory_space=pltpu.SMEM)
    whole = lambda x: pl.BlockSpec(x.shape, lambda l: (0,) * x.ndim)
    tile = pl.BlockSpec((per, lc, BS, BS), lambda l: (l, 0, 0, 0))
    return pl.pallas_call(
        schur_kernel,
        grid=(lr // per,),
        out_shape=jax.ShapeDtypeStruct(blocks.shape, F32),
        in_specs=[smem, smem]
        + [whole(x) for x in (*inverse, rows, cols, panel, landed, *solved)]
        + [tile]
        + [whole(x) for x in (*mine, *other)],
        out_specs=tile,
        scratch_shapes=[
            pltpu.VMEM((PB, per * BS, BS), F32),
            pltpu.VMEM((per * BS, PW), BF16),
            pltpu.VMEM((per * BS, PW), BF16),
            pltpu.VMEM((per * BS, PW), F32),
            pltpu.VMEM((512, 256), F32),
            pltpu.VMEM((2, 256, PW), BF16),
        ],
        compiler_params=pltpu.CompilerParams(vmem_limit_bytes=60 << 20),
        cost_estimate=pl.CostEstimate(
            flops=16_000_000_000, bytes_accessed=24 << 20, transcendentals=0
        ),
        name="schur_update",
    )(place, pattern, *inverse, rows, cols, panel, landed, *solved, blocks, *mine, *other)


def after(x, *first):
    return lax.optimization_barrier((x,) + first)[0]


def scatter_quarters(quarters, col):
    got = jnp.where(col < PB, quarters[0], 0.0)
    for q in range(1, 4):
        got = got + lax.ppermute(quarters[q], "col", [(k, HOLDER[k][q]) for k in range(PB)])
    return got


def shift_plane(x, dx, dy):
    pairs = []
    for c in range(16):
        at_x, at_y, core = c // 8, (c // 2) % 4, c % 2
        pairs.append((c, ((at_x + dx) % 2) * 8 + ((at_y + dy) % 4) * 2 + core))
    return lax.ppermute(x, "col", pairs)


def gather_corner(piece):
    both = jnp.stack([piece, shift_plane(piece, 1, 0)])
    up, down = shift_plane(both, 0, 1), shift_plane(both, 0, 3)
    return [both, up, down, shift_plane(up[0], 0, 1), shift_plane(down[1], 0, 3)]


def gather_panel(piece):
    both = jnp.stack([piece, shift_plane(piece, 1, 0)])
    return [both] + [shift_plane(both, 0, dy) for dy in (1, 2, 3)]


def swap_cores(pieces):
    return [lax.ppermute(x, "col", [(c, c ^ 1) for c in range(16)]) for x in pieces]


def shift_row(x, d):
    return lax.ppermute(x, "row", [(z, (z + d) % 8) for z in range(8)])


def per_device(front, child_update, child_map, pattern):
    row = lax.axis_index("row")
    col = lax.axis_index("col")
    place = jnp.stack([row, col, col % 2, (col // 2) % 4, col // 8]).astype(jnp.int32)
    blocks = front[0].transpose(0, 2, 1, 3)
    lr, lc = blocks.shape[:2]
    msg, corner_child, part, rows, cols, lanes, panel_sub, panel_lanes = pack(
        place, child_map[0].reshape(16, 128), child_update[0]
    )

    first = blocks[0, 0]
    first = scatter_quarters([first[q * QUARTER:(q + 1) * QUARTER] for q in range(4)], col)
    corner = jnp.concatenate([first, corner_child], axis=0)
    came = [corner] + [shift_row(corner, d) for d in range(1, 8)]
    corner = []
    for d in range(PB):
        here = (row - d) % 8 < PB
        low, high = jnp.where(here, came[d], came[d + 4]), jnp.where(here, came[d + 4], came[d])
        corner.append(jnp.concatenate([low, high[QUARTER:]], axis=0))
    corner = jnp.stack(corner)
    corner_mine = gather_corner(corner)
    corner_other = swap_cores(corner_mine)
    inverse = corner_inverse(place, panel_sub, panel_lanes, corner_mine, corner_other)

    lead = after(blocks[:, 0], first).reshape(lr, 4, QUARTER, BS)
    own = scatter_quarters([lead[:, q] for q in range(4)], col)
    sent = own.reshape(lr, 8, 8, BS).transpose(1, 0, 2, 3).reshape(8, lr * 8, BS)
    sent = after(jnp.concatenate([sent, msg], axis=1), corner_mine[0])
    sent = lax.all_to_all(sent, "row", split_axis=0, concat_axis=0, tiled=True)
    turned = turn(sent[:, lr * 8:])
    strips = sent[:, :lr * 8].reshape(8, lc, 2, 8, BS).transpose(2, 0, 1, 3, 4)
    sent = jnp.concatenate(
        [strips.reshape(16, lc * 8, BS), turned.reshape(16, 8, BS), part], axis=1
    )
    sent = after(sent, corner_mine[1], corner_mine[2])
    sent = lax.all_to_all(sent, "col", split_axis=0, concat_axis=0, tiled=True)
    landed = sent[:, lc * 8:lc * 8 + 8].reshape(128, 256)
    held = jnp.concatenate(
        [
            sent[:, :lc * 8].reshape(16 * lc * 8, BS),
            sent[:, lc * 8 + 8:].reshape(4, 4, 8, BS).sum(1).reshape(32, BS),
        ],
        axis=0,
    )
    held = lax.all_gather(held, "row", axis=0, tiled=False)

    own = jnp.concatenate([own.reshape(lr * QUARTER, BS), turned[:32]], axis=0)
    panel_mine = gather_panel(own)
    panel_other = swap_cores(panel_mine[:1] + [after(x, inverse[0]) for x in panel_mine[1:]])
    solved = solved_columns(inverse, lanes, panel_sub, held, lc)
    out = schur_update(
        place, pattern[0], inverse, rows, cols, panel_sub, landed, solved, blocks, panel_mine, panel_other
    )
    return out.transpose(0, 2, 1, 3)[None]


def solution(mesh):
    placed = (
        P("front", None, "row", None, "col"),
        P("front", "row", "col"),
        P("front", None),
        P("front", None, None),
    )
    return jax.shard_map(
        per_device,
        mesh=mesh,
        in_specs=placed,
        out_specs=P("front", None, "row", None, "col"),
        check_vma=False,
    )
```

```python
import functools

import jax
import jax.numpy as jnp
from jax import lax
from jax.experimental import pallas as pl
from jax.experimental.pallas import tpu as pltpu
from jax.sharding import PartitionSpec as P

BS = 256
PB = 4
PW = 1024
KB = 128
F32 = jnp.float32
BF16 = jnp.bfloat16
HIGHEST = lax.Precision.HIGHEST
QUARTER = BS // 4

HOLDER = ((0, 6, 8, 14), (1, 7, 9, 15), (2, 4, 10, 12), (3, 5, 11, 13))
CORNER_SHIFTS = (
    (0, 0, 0, 0), (1, 0, 0, 1), (0, 1, 1, 0), (1, 1, 1, 1),
    (0, 3, 2, 0), (1, 3, 2, 1), (0, 2, 3, None), (1, 2, 4, None),
)
PANEL_SHIFTS = tuple((dx, dy, dy, dx) for dy in range(4) for dx in range(2))


def nn(a, b, precision=None):
    return lax.dot_general(
        a, b, (((1,), (0,)), ((), ())), precision=precision, preferred_element_type=F32
    )


def nt(a, b, precision=None):
    return lax.dot_general(
        a, b, (((1,), (1,)), ((), ())), precision=precision, preferred_element_type=F32
    )


def iota(shape, dim):
    return lax.broadcasted_iota(jnp.int32, shape, dim)


def split2(x):
    high = x.astype(BF16)
    return high, (x - high.astype(F32)).astype(BF16)


def split3(x):
    high = x.astype(BF16)
    rest = x - high.astype(F32)
    middle = rest.astype(BF16)
    return high, middle, (rest - middle.astype(F32)).astype(BF16)


def pack_kernel(
    place, map_ref, update_ref, msg_ref, corner_ref, part_ref,
    rows_ref, cols_ref, lanes_ref, panel_ref, panel_lanes_ref, rank_s, class_s, turned_s,
):
    row, col = place[0], place[1]
    mapping = map_ref[...]
    owner = (mapping >> 8) & 15
    hot = (iota((16, 16, 128), 1) == owner[:, None, :]).astype(F32)
    before = (iota((128, 128), 0) < iota((128, 128), 1)).astype(F32).astype(BF16)
    counts = nn(hot.reshape(256, 128).astype(BF16), before).reshape(16, 16, 128)
    rank = jnp.sum(hot * counts, axis=1).astype(jnp.int32)
    rank_s[...] = rank
    class_s[...] = owner
    slot = owner * 8 + rank
    col_slot = class_s[pl.ds(col, 1), :] * 8 + rank_s[pl.ds(col, 1), :]
    col_hot = (iota((128, 128), 0) == col_slot).astype(F32)
    row_hot = []
    for run in range(2):
        this = class_s[pl.ds(2 * row + run, 1), :]
        row_slot = (this & 7) * 32 + run * 16 + (this >> 3) * 8 + rank_s[pl.ds(2 * row + run, 1), :]
        row_hot.append((iota((256, 128), 0) == row_slot).astype(F32))
    moved = nt(update_ref[...], col_hot, HIGHEST)
    moved = nn(jnp.concatenate(row_hot, axis=1), moved, HIGHEST)
    part_ref[...] = jnp.zeros((16, 8, 256), F32)
    for r in range(8):
        for half in range(2):
            msg_ref[r, :, half * 128:(half + 1) * 128] = moved[
                r * 32 + half * 16:r * 32 + half * 16 + 16, :
            ]
        for run in range(2):
            for upper in range(2):
                at = r * 32 + run * 16 + upper * 8
                piece = moved[at:at + 8, 0:32]
                if upper == 0 and r < PB:
                    g = run * 4 + r
                    corner_ref[:, g * 32:(g + 1) * 32] = piece
                for slot_lane in range(4):

                    @pl.when((col & 3) == slot_lane)
                    def _():
                        lo = run * 128 + slot_lane * 32
                        part_ref[upper * 8 + r, :, lo:lo + 32] = piece

    parts = jnp.concatenate([mapping >> 7, mapping & 127], axis=0).astype(F32).astype(BF16)
    ordered = jnp.zeros((16, 128), F32)
    for run in range(16):
        run_hot = (iota((128, 128), 0) == slot[run:run + 1, :]).astype(F32).astype(BF16)
        moved_map = nt(parts, run_hot)
        both_parts = moved_map[:16] * 128.0 + moved_map[16:]
        ordered = jnp.where(iota((16, 128), 0) == run, both_parts, ordered)
    turned_s[...] = jnp.concatenate([ordered, jnp.zeros((112, 128), F32)], axis=0).T
    mine = turned_s[pl.ds(pl.multiple_of(col * 8, 8), 8), :]
    lead = turned_s[0:32, :]
    for run in range(16):
        cols_ref[run * 8:(run + 1) * 8, :] = jnp.broadcast_to(
            mine[:, run:run + 1], (8, 128)
        ).astype(jnp.int32)
        panel_ref[run * 32:(run + 1) * 32, :] = jnp.broadcast_to(
            lead[:, run:run + 1], (32, 128)
        ).astype(jnp.int32)
    whole = ordered.astype(jnp.int32)
    parts = jnp.concatenate([whole >> 7, whole & 127], axis=0).astype(F32).astype(BF16)

    def spread(ref, width, slot_of, run_of):
        lane = iota((128, width), 1)
        pick = (iota((128, width), 0) == slot_of(lane)).astype(F32).astype(BF16)
        value = nn(parts, pick)
        value = value[:16] * 128.0 + value[16:]
        value = jnp.where(run_of(iota((16, width), 1)) == iota((16, width), 0), value, 0.0)
        ref[...] = jnp.broadcast_to(jnp.sum(value, axis=0, keepdims=True), (8, width)).astype(
            jnp.int32
        )

    spread(rows_ref, 256, lambda n: (((n >> 3) & 1) * 8 + row) * 8 + (n & 7), lambda n: n >> 4)
    spread(lanes_ref, 128, lambda n: col * 8 + (n & 7), lambda n: n >> 3)
    spread(panel_lanes_ref, 512, lambda n: n & 31, lambda n: n >> 5)


def pack(place, mapping, update):
    smem = pl.BlockSpec(memory_space=pltpu.SMEM)
    vmem = pl.BlockSpec(memory_space=pltpu.VMEM)
    ints = lambda *shape: jax.ShapeDtypeStruct(shape, jnp.int32)
    return pl.pallas_call(
        pack_kernel,
        out_shape=(
            jax.ShapeDtypeStruct((8, 16, 256), F32),
            jax.ShapeDtypeStruct((8, 256), F32),
            jax.ShapeDtypeStruct((16, 8, 256), F32),
            ints(8, 256),
            ints(128, 128),
            ints(8, 128),
            ints(512, 128),
            ints(8, 512),
        ),
        in_specs=[smem, vmem, vmem],
        out_specs=(vmem,) * 8,
        scratch_shapes=[
            pltpu.VMEM((16, 128), jnp.int32),
            pltpu.VMEM((16, 128), jnp.int32),
            pltpu.VMEM((128, 128), F32),
        ],
        name="pack",
    )(place, mapping, update)


def turn_kernel(recv_ref, out_ref):
    pieces = []
    for r in range(8):
        pieces += [recv_ref[r, :, 0:128], recv_ref[r, :, 128:256]]
    out_ref[...] = jnp.concatenate(pieces, axis=0).T


def turn(recv):
    vmem = pl.BlockSpec(memory_space=pltpu.VMEM)
    return pl.pallas_call(
        turn_kernel,
        out_shape=jax.ShapeDtypeStruct((128, 256), F32),
        in_specs=[vmem],
        out_specs=vmem,
        name="turn",
    )(recv)


def row_place(g):
    return ((g >> 11) << 8) + (g & 255)


def col_place(g):
    return ((g >> 12) << 8) + (g & 255)


def as_hot(mask):
    return mask.astype(F32).astype(BF16)


def factor_inverse(block):
    a = [block[8 * s:8 * s + 8, :] for s in range(16)]
    sub, lane = iota((8, 128), 0), iota((8, 128), 1)
    lanes_of = lambda x, j: jnp.broadcast_to(x[:, j:j + 1], (8, 128))
    row_of = lambda x, i: jnp.broadcast_to(x[i:i + 1, :], (8, 128))
    for s in range(16):
        js = [8 * s + q for q in range(8)]
        c = [lanes_of(a[s], j) for j in js]
        strip = a[s]
        rows, mult = [], [[None] * 8 for _ in range(8)]
        pivots = jnp.zeros((8, 128), F32)
        for q in range(8):
            pivot = row_of(c[q], q)
            over = 1.0 / pivot
            pivots = jnp.where(sub == q, pivot, pivots)
            below = jnp.where(sub > q, c[q], 0.0)
            strip = jnp.where(lane == js[q], jnp.where(sub == q, 1.0, 0.0), strip)
            row = row_of(strip, q) * over
            rows.append(jnp.where((lane <= js[q]) | (lane > js[7]), row, 0.0))
            for q2 in range(q + 1, 8):
                m = row_of(c[q2], q) * over
                mult[q][q2] = m
                c[q2] = c[q2] - below * m
            strip = strip - below * row
        a[s] = jnp.where(lane <= sub + 8 * s, strip, 0.0) * lax.rsqrt(pivots)
        kept = (lane < js[0]) | (lane > js[7])
        for t in range(s + 1, 16):
            ct = [lanes_of(a[t], j) for j in js]
            for q in range(8):
                for q2 in range(q + 1, 8):
                    ct[q2] = ct[q2] - ct[q] * mult[q][q2]
            value = jnp.where(kept, a[t], 0.0)
            for q in range(8):
                value = value - ct[q] * rows[q]
            a[t] = value
    return jnp.concatenate(a, axis=0)


def holders(place, mine, other, shifts):
    core, y, x = place[2], place[3], place[4]
    for refs, at_core in ((mine, core), (other, 1 - core)):
        for dx, dy, index, part in shifts:
            ref = refs[index] if part is None else refs[index].at[part]
            from_x, from_y = (x - dx) & 1, (y - dy) & 3
            middle = ((from_y + 1) >> 1) & 1
            yield ref, from_x * 8 + from_y * 2 + at_core, at_core + 2 * middle, from_x * 2 + (from_y >> 1)


def corner_kernel(place, panel_ref, lanes_ref, *refs):
    mine, other = refs[:5], refs[5:10]
    high_ref, low_ref, inv_ref, s_ref, raw_s, child_s, placed_s = refs[10:]
    n, b = PW // KB, KB
    row = place[0]
    slot_of = iota((8, 128), 1) >> 5
    for ref, holder, k, q in holders(place, mine, other, CORNER_SHIFTS):
        for block in range(PB):
            start = pl.multiple_of(block * BS + q * QUARTER, QUARTER)
            raw_s[k, pl.ds(start, QUARTER), :] = ref[(row - block) & 3, 0:QUARTER, :]
        lane_slot = holder & 3
        for block in range(2 * PB):
            at = QUARTER + (block // PB) * 8
            for half in range(2):
                value = ref[(row - block) & 3, at:at + 8, half * 128:(half + 1) * 128]
                for g in range(4):
                    start = (block * 2 + half) * 32 + g * 8
                    shifted = pltpu.roll(value, ((lane_slot - g) & 3) * 32, 1)
                    old = child_s[holder >> 2, start:start + 8, :]
                    child_s[holder >> 2, start:start + 8, :] = jnp.where(
                        slot_of == lane_slot, shifted, old
                    )
    child = jnp.concatenate([child_s[i] for i in range(4)], axis=1)
    child = 0.5 * (child + child.T)
    col_hot = as_hot(panel_ref[:, 0:1] == iota((512, PW), 1))
    placed_s[...] = sum(nn(part, col_hot) for part in split3(child))
    lanes = lanes_ref[0:1, :]
    raw = lambda i, j: raw_s[j // 2, i * b:(i + 1) * b, (j % 2) * b:(j % 2 + 1) * b]
    for i in range(n):
        row_hot = as_hot(iota((b, 512), 0) + i * b == lanes)
        added = sum(nn(row_hot, part) for part in split3(placed_s[:, :(i + 1) * b]))
        for j in range(i + 1):
            s_ref[i * b:(i + 1) * b, j * b:(j + 1) * b] = (
                0.5 * (raw(i, j) + raw(j, i).T) + added[:, j * b:(j + 1) * b]
            )
    for k in range(n):
        lo, hi = k * b, (k + 1) * b
        diag = factor_inverse(s_ref[lo:hi, lo:hi])
        if k < n - 1:
            below = nt(s_ref[hi:, lo:hi], diag, HIGHEST)
            s_ref[hi:, hi:hi + b] = s_ref[hi:, hi:hi + b] - nt(below, below[:b], HIGHEST)
        if k > 0:
            left = nn(diag, inv_ref[lo:hi, :lo], HIGHEST)
            inv_ref[lo:hi, :lo] = left
        inv_ref[lo:hi, lo:hi] = diag
        high_ref[lo:hi, :hi], low_ref[lo:hi, :hi] = split2(inv_ref[lo:hi, :hi])
        if k % 2 == 0:
            high_ref[lo:hi, hi:hi + b] = jnp.zeros((b, b), BF16)
            low_ref[lo:hi, hi:hi + b] = jnp.zeros((b, b), BF16)
        if k < n - 1:
            for j in range(k + 2, n):
                at = (j - k - 1) * b
                s_ref[j * b:, j * b:(j + 1) * b] = s_ref[j * b:, j * b:(j + 1) * b] - nt(
                    below[at:], below[at:at + b], HIGHEST
                )
            if k > 0:
                inv_ref[hi:, :lo] = inv_ref[hi:, :lo] - nn(below, left, HIGHEST)
            inv_ref[hi:, lo:hi] = -nn(below, diag, HIGHEST)


def corner_inverse(place, panel, lanes, mine, other):
    smem = pl.BlockSpec(memory_space=pltpu.SMEM)
    vmem = pl.BlockSpec(memory_space=pltpu.VMEM)
    return pl.pallas_call(
        corner_kernel,
        out_shape=(jax.ShapeDtypeStruct((PW, PW), BF16),) * 2,
        in_specs=[smem] + [vmem] * 12,
        out_specs=(vmem, vmem),
        scratch_shapes=[
            pltpu.VMEM((PW, PW), F32),
            pltpu.VMEM((PW, PW), F32),
            pltpu.VMEM((PB, PW, BS), F32),
            pltpu.VMEM((4, 512, 128), F32),
            pltpu.VMEM((512, PW), F32),
        ],
        compiler_params=pltpu.CompilerParams(vmem_limit_bytes=48 << 20),
        cost_estimate=pl.CostEstimate(
            flops=40_000_000_000, bytes_accessed=8 << 20, transcendentals=0
        ),
        name="corner_inverse",
    )(place, panel, lanes, *mine, *other)


def three_pass(a, b):
    return nt(a[0], b[0]) + nt(a[0], b[1]) + nt(a[1], b[0])


def schur_kernel(
    place, pattern, inv_h, inv_l, rows_ref, cols_ref, lanes_ref, panel_ref, landed_ref, held_ref, front_ref, *refs
):
    mine, other = refs[:4], refs[4:8]
    (out_ref, raw_s, col_h, col_l, row_h, row_l, row_f, child_s, child_p) = refs[8:]
    row, col = place[0], place[1]
    step = pl.program_id(0)
    per, lc = out_ref.shape[:2]

    def solve(raw, high_ref, low_ref, full_ref=None):
        raw = split2(raw)
        for j in range(PB):
            lo, deep = j * BS, (j + 1) * BS
            value = three_pass(
                (raw[0][:, :deep], raw[1][:, :deep]), (inv_h[lo:deep, :deep], inv_l[lo:deep, :deep])
            )
            high_ref[:, lo:deep], low_ref[:, lo:deep] = split2(value)
            if full_ref is not None:
                full_ref[:, lo:deep] = value

    @pl.when(step == 0)
    def _():
        col_hot = as_hot(panel_ref[:, 0:1] == iota((512, PW), 1))
        held_child = []
        for run in range(16):
            held_child.append(
                jnp.concatenate(
                    [
                        held_ref[run // 2, 384 + g * 8:392 + g * 8, (run % 2) * 128:(run % 2 + 1) * 128]
                        for g in range(4)
                    ],
                    axis=1,
                )
            )
        held_child = jnp.concatenate(held_child, axis=0)
        placed = split2(sum(nn(part, col_hot) for part in split2(held_child)))
        raw = []
        for k in range(PB):
            column = []
            for m in range(lc):
                for q in range(4):
                    at = HOLDER[k][q] * 24 + m * 8
                    column += [held_ref[r, at:at + 8, :] for r in range(8)]
            raw.append(jnp.concatenate(column, axis=0))
        raw = jnp.concatenate(raw, axis=1)
        row_hot = as_hot(iota((lc * BS, 128), 0) == col_place(lanes_ref[0:1, :]))
        solve(raw + sum(nn(row_hot, part) for part in placed), col_h, col_l)
        for ref, holder, k, q in holders(place, mine, other, PANEL_SHIFTS):
            child_s[pl.ds(pl.multiple_of(holder * 32, 32), 32), :] = ref[384:416, :]
        placed = sum(nn(part, col_hot) for part in split2(child_s[...].T))
        child_p[0], child_p[1] = split2(placed)

    for ref, holder, k, q in holders(place, mine, other, PANEL_SHIFTS):
        for h in range(per):
            start = pl.multiple_of(h * BS + q * QUARTER, QUARTER)
            at = pl.multiple_of((step * per + h) * QUARTER, QUARTER)
            raw_s[k, pl.ds(start, QUARTER), :] = ref[pl.ds(at, QUARTER), :]
    row_hot = as_hot(
        iota((per * BS, 256), 0) + step * (per * BS) == row_place(rows_ref[0:1, :])
    )
    raw_rows = jnp.concatenate([raw_s[k] for k in range(PB)], axis=1)
    raw_rows = raw_rows + nn(row_hot, child_p[0]) + nn(row_hot, child_p[1])
    solve(raw_rows, row_h, row_l, row_f)

    added = split3(sum(nt(row_hot, part) for part in split3(landed_ref[...])))
    for m in range(lc):
        col_hot = as_hot(col_place(cols_ref[:, 0:1]) == iota((128, BS), 1) + m * BS)
        e = sum(nn(part, col_hot) for part in added)
        block_col = m * 16 + col
        for h in range(per):
            block_row = (step * per + h) * 8 + row
            at = slice(h * BS, (h + 1) * BS)
            out_ref[h, m] = front_ref[h, m] + e[at]
            applied = (pattern[block_row, block_col] == 1) & (block_row >= PB) & (block_col >= PB)

            @pl.when(applied)
            def _():
                out_ref[h, m] = out_ref[h, m] - three_pass(
                    (row_h[at], row_l[at]),
                    (col_h[m * BS:(m + 1) * BS], col_l[m * BS:(m + 1) * BS]),
                )

    @pl.when(col < PB)
    def _():
        start = pl.multiple_of(jnp.minimum(col, PB - 1) * BS, BS)
        for h in range(per):
            out_ref[h, 0] = row_f[h * BS:(h + 1) * BS, pl.ds(start, BS)]


def schur_update(place, pattern, inverse, rows, cols, lanes, panel, landed, held, blocks, mine, other):
    lr, lc = blocks.shape[:2]
    per = 2
    smem = pl.BlockSpec(memory_space=pltpu.SMEM)
    whole = lambda x: pl.BlockSpec(x.shape, lambda l: (0,) * x.ndim)
    tile = pl.BlockSpec((per, lc, BS, BS), lambda l: (l, 0, 0, 0))
    return pl.pallas_call(
        schur_kernel,
        grid=(lr // per,),
        out_shape=jax.ShapeDtypeStruct(blocks.shape, F32),
        in_specs=[smem, smem]
        + [whole(x) for x in (*inverse, rows, cols, lanes, panel, landed, held)]
        + [tile]
        + [whole(x) for x in (*mine, *other)],
        out_specs=tile,
        scratch_shapes=[
            pltpu.VMEM((PB, per * BS, BS), F32),
            pltpu.VMEM((lc * BS, PW), BF16),
            pltpu.VMEM((lc * BS, PW), BF16),
            pltpu.VMEM((per * BS, PW), BF16),
            pltpu.VMEM((per * BS, PW), BF16),
            pltpu.VMEM((per * BS, PW), F32),
            pltpu.VMEM((512, 256), F32),
            pltpu.VMEM((2, 256, PW), BF16),
        ],
        compiler_params=pltpu.CompilerParams(vmem_limit_bytes=60 << 20),
        cost_estimate=pl.CostEstimate(
            flops=16_000_000_000, bytes_accessed=24 << 20, transcendentals=0
        ),
        name="schur_update",
    )(place, pattern, *inverse, rows, cols, lanes, panel, landed, held, blocks, *mine, *other)


def after(x, *first):
    return lax.optimization_barrier((x,) + first)[0]


def scatter_quarters(quarters, col):
    got = jnp.where(col < PB, quarters[0], 0.0)
    for q in range(1, 4):
        got = got + lax.ppermute(quarters[q], "col", [(k, HOLDER[k][q]) for k in range(PB)])
    return got


def shift_plane(x, dx, dy):
    pairs = []
    for c in range(16):
        at_x, at_y, core = c // 8, (c // 2) % 4, c % 2
        pairs.append((c, ((at_x + dx) % 2) * 8 + ((at_y + dy) % 4) * 2 + core))
    return lax.ppermute(x, "col", pairs)


def gather_corner(piece):
    both = jnp.stack([piece, shift_plane(piece, 1, 0)])
    up, down = shift_plane(both, 0, 1), shift_plane(both, 0, 3)
    return [both, up, down, shift_plane(up[0], 0, 1), shift_plane(down[1], 0, 3)]


def gather_panel(piece):
    both = jnp.stack([piece, shift_plane(piece, 1, 0)])
    return [both] + [shift_plane(both, 0, dy) for dy in (1, 2, 3)]


def swap_cores(pieces):
    return [lax.ppermute(x, "col", [(c, c ^ 1) for c in range(16)]) for x in pieces]


def shift_row(x, d):
    return lax.ppermute(x, "row", [(z, (z + d) % 8) for z in range(8)])


def per_device(front, child_update, child_map, pattern):
    row = lax.axis_index("row")
    col = lax.axis_index("col")
    place = jnp.stack([row, col, col % 2, (col // 2) % 4, col // 8]).astype(jnp.int32)
    blocks = front[0].transpose(0, 2, 1, 3)
    lr, lc = blocks.shape[:2]
    msg, corner_child, part, rows, cols, lanes, panel_sub, panel_lanes = pack(
        place, child_map[0].reshape(16, 128), child_update[0]
    )

    first = blocks[0, 0]
    first = scatter_quarters([first[q * QUARTER:(q + 1) * QUARTER] for q in range(4)], col)
    corner = jnp.concatenate([first, corner_child], axis=0)
    came = [corner] + [shift_row(corner, d) for d in range(1, 8)]
    corner = []
    for d in range(PB):
        here = (row - d) % 8 < PB
        low, high = jnp.where(here, came[d], came[d + 4]), jnp.where(here, came[d + 4], came[d])
        corner.append(jnp.concatenate([low, high[QUARTER:]], axis=0))
    corner = jnp.stack(corner)
    corner_mine = gather_corner(corner)
    over_planes = corner
    corner_other = swap_cores(corner_mine)
    inverse = corner_inverse(place, panel_sub, panel_lanes, corner_mine, corner_other)

    lead = after(blocks[:, 0], first).reshape(lr, 4, QUARTER, BS)
    own = scatter_quarters([lead[:, q] for q in range(4)], col)
    sent = own.reshape(lr, 8, 8, BS).transpose(1, 0, 2, 3).reshape(8, lr * 8, BS)
    sent = after(jnp.concatenate([sent, msg], axis=1), over_planes)
    sent = lax.all_to_all(sent, "row", split_axis=0, concat_axis=0, tiled=True)
    turned = turn(sent[:, lr * 8:])
    strips = sent[:, :lr * 8].reshape(8, lc, 2, 8, BS).transpose(2, 0, 1, 3, 4)
    sent = jnp.concatenate(
        [strips.reshape(16, lc * 8, BS), turned.reshape(16, 8, BS), part], axis=1
    )
    sent = after(sent, corner_mine[3], corner_mine[4])
    sent = lax.all_to_all(sent, "col", split_axis=0, concat_axis=0, tiled=True)
    landed = sent[:, lc * 8:lc * 8 + 8].reshape(128, 256)
    held = jnp.concatenate(
        [
            sent[:, :lc * 8].reshape(16 * lc * 8, BS),
            sent[:, lc * 8 + 8:].reshape(4, 4, 8, BS).sum(1).reshape(32, BS),
        ],
        axis=0,
    )
    held = lax.all_gather(held, "row", axis=0, tiled=False)

    own = jnp.concatenate([own.reshape(lr * QUARTER, BS), turned[:32]], axis=0)
    own = after(own, corner_mine[3], corner_mine[4])
    panel_mine = gather_panel(own)
    panel_other = swap_cores(panel_mine[:1] + [after(x, inverse[0]) for x in panel_mine[1:]])
    out = schur_update(
        place, pattern[0], inverse, rows, cols, lanes, panel_sub, landed, held, blocks,
        panel_mine, panel_other,
    )
    return out.transpose(0, 2, 1, 3)[None]


def solution(mesh):
    placed = (
        P("front", None, "row", None, "col"),
        P("front", "row", "col"),
        P("front", None),
        P("front", None, None),
    )
    return jax.shard_map(
        per_device,
        mesh=mesh,
        in_specs=placed,
        out_specs=P("front", None, "row", None, "col"),
        check_vma=False,
    )
```

```python
import functools

import jax
import jax.numpy as jnp
from jax import lax
from jax.experimental import pallas as pl
from jax.experimental.pallas import tpu as pltpu
from jax.sharding import PartitionSpec as P

BS = 256
PB = 4
PW = 1024
KB = 128
F32 = jnp.float32
BF16 = jnp.bfloat16
HIGHEST = lax.Precision.HIGHEST
QUARTER = BS // 4

HOLDER = ((0, 6, 8, 14), (1, 7, 9, 15), (2, 4, 10, 12), (3, 5, 11, 13))
PLANE_SHIFTS = tuple((dx, dy, dy, dx) for dy in range(4) for dx in range(2))


def nn(a, b, precision=None):
    return lax.dot_general(
        a, b, (((1,), (0,)), ((), ())), precision=precision, preferred_element_type=F32
    )


def nt(a, b, precision=None):
    return lax.dot_general(
        a, b, (((1,), (1,)), ((), ())), precision=precision, preferred_element_type=F32
    )


def iota(shape, dim):
    return lax.broadcasted_iota(jnp.int32, shape, dim)


def split2(x):
    high = x.astype(BF16)
    return high, (x - high.astype(F32)).astype(BF16)


def split3(x):
    high = x.astype(BF16)
    rest = x - high.astype(F32)
    middle = rest.astype(BF16)
    return high, middle, (rest - middle.astype(F32)).astype(BF16)


def pack_kernel(
    place, map_ref, update_ref, msg_ref, corner_ref, part_ref,
    rows_ref, cols_ref, lanes_ref, panel_ref, panel_lanes_ref, rank_s, class_s, turned_s,
):
    row, col = place[0], place[1]
    mapping = map_ref[...]
    owner = (mapping >> 8) & 15
    hot = (iota((16, 16, 128), 1) == owner[:, None, :]).astype(F32)
    before = (iota((128, 128), 0) < iota((128, 128), 1)).astype(F32).astype(BF16)
    counts = nn(hot.reshape(256, 128).astype(BF16), before).reshape(16, 16, 128)
    rank = jnp.sum(hot * counts, axis=1).astype(jnp.int32)
    rank_s[...] = rank
    class_s[...] = owner
    slot = owner * 8 + rank
    col_slot = class_s[pl.ds(col, 1), :] * 8 + rank_s[pl.ds(col, 1), :]
    col_hot = (iota((128, 128), 0) == col_slot).astype(F32)
    row_hot = []
    for run in range(2):
        this = class_s[pl.ds(2 * row + run, 1), :]
        row_slot = (this & 7) * 32 + run * 16 + (this >> 3) * 8 + rank_s[pl.ds(2 * row + run, 1), :]
        row_hot.append((iota((256, 128), 0) == row_slot).astype(F32))
    moved = nt(update_ref[...], col_hot, HIGHEST)
    moved = nn(jnp.concatenate(row_hot, axis=1), moved, HIGHEST)
    part_ref[...] = jnp.zeros((16, 8, 256), F32)
    for r in range(8):
        for half in range(2):
            msg_ref[r, :, half * 128:(half + 1) * 128] = moved[
                r * 32 + half * 16:r * 32 + half * 16 + 16, :
            ]
        for run in range(2):
            for upper in range(2):
                at = r * 32 + run * 16 + upper * 8
                piece = moved[at:at + 8, 0:32]
                if upper == 0 and r < PB:
                    g = run * 4 + r
                    corner_ref[:, g * 32:(g + 1) * 32] = piece
                for slot_lane in range(4):

                    @pl.when((col & 3) == slot_lane)
                    def _():
                        lo = run * 128 + slot_lane * 32
                        part_ref[upper * 8 + r, :, lo:lo + 32] = piece

    parts = jnp.concatenate([mapping >> 7, mapping & 127], axis=0).astype(F32).astype(BF16)
    ordered = jnp.zeros((16, 128), F32)
    for run in range(16):
        run_hot = (iota((128, 128), 0) == slot[run:run + 1, :]).astype(F32).astype(BF16)
        moved_map = nt(parts, run_hot)
        both_parts = moved_map[:16] * 128.0 + moved_map[16:]
        ordered = jnp.where(iota((16, 128), 0) == run, both_parts, ordered)
    turned_s[...] = jnp.concatenate([ordered, jnp.zeros((112, 128), F32)], axis=0).T
    mine = turned_s[pl.ds(pl.multiple_of(col * 8, 8), 8), :]
    lead = turned_s[0:32, :]
    for run in range(16):
        cols_ref[run * 8:(run + 1) * 8, :] = jnp.broadcast_to(
            mine[:, run:run + 1], (8, 128)
        ).astype(jnp.int32)
        panel_ref[run * 32:(run + 1) * 32, :] = jnp.broadcast_to(
            lead[:, run:run + 1], (32, 128)
        ).astype(jnp.int32)
    whole = ordered.astype(jnp.int32)
    parts = jnp.concatenate([whole >> 7, whole & 127], axis=0).astype(F32).astype(BF16)

    def spread(ref, width, slot_of, run_of):
        lane = iota((128, width), 1)
        pick = (iota((128, width), 0) == slot_of(lane)).astype(F32).astype(BF16)
        value = nn(parts, pick)
        value = value[:16] * 128.0 + value[16:]
        value = jnp.where(run_of(iota((16, width), 1)) == iota((16, width), 0), value, 0.0)
        ref[...] = jnp.broadcast_to(jnp.sum(value, axis=0, keepdims=True), (8, width)).astype(
            jnp.int32
        )

    spread(rows_ref, 256, lambda n: (((n >> 3) & 1) * 8 + row) * 8 + (n & 7), lambda n: n >> 4)
    spread(lanes_ref, 128, lambda n: col * 8 + (n & 7), lambda n: n >> 3)
    spread(panel_lanes_ref, 512, lambda n: n & 31, lambda n: n >> 5)


def pack(place, mapping, update):
    smem = pl.BlockSpec(memory_space=pltpu.SMEM)
    vmem = pl.BlockSpec(memory_space=pltpu.VMEM)
    ints = lambda *shape: jax.ShapeDtypeStruct(shape, jnp.int32)
    return pl.pallas_call(
        pack_kernel,
        out_shape=(
            jax.ShapeDtypeStruct((8, 16, 256), F32),
            jax.ShapeDtypeStruct((8, 256), F32),
            jax.ShapeDtypeStruct((16, 8, 256), F32),
            ints(8, 256),
            ints(128, 128),
            ints(8, 128),
            ints(512, 128),
            ints(8, 512),
        ),
        in_specs=[smem, vmem, vmem],
        out_specs=(vmem,) * 8,
        scratch_shapes=[
            pltpu.VMEM((16, 128), jnp.int32),
            pltpu.VMEM((16, 128), jnp.int32),
            pltpu.VMEM((128, 128), F32),
        ],
        name="pack",
    )(place, mapping, update)


def turn_kernel(recv_ref, out_ref):
    pieces = []
    for r in range(8):
        pieces += [recv_ref[r, :, 0:128], recv_ref[r, :, 128:256]]
    out_ref[...] = jnp.concatenate(pieces, axis=0).T


def turn(recv):
    vmem = pl.BlockSpec(memory_space=pltpu.VMEM)
    return pl.pallas_call(
        turn_kernel,
        out_shape=jax.ShapeDtypeStruct((128, 256), F32),
        in_specs=[vmem],
        out_specs=vmem,
        name="turn",
    )(recv)


def row_place(g):
    return ((g >> 11) << 8) + (g & 255)


def col_place(g):
    return ((g >> 12) << 8) + (g & 255)


def as_hot(mask):
    return mask.astype(F32).astype(BF16)


def factor_inverse(block):
    a = [block[8 * s:8 * s + 8, :] for s in range(16)]
    sub, lane = iota((8, 128), 0), iota((8, 128), 1)
    lanes_of = lambda x, j: jnp.broadcast_to(x[:, j:j + 1], (8, 128))
    row_of = lambda x, i: jnp.broadcast_to(x[i:i + 1, :], (8, 128))
    for s in range(16):
        js = [8 * s + q for q in range(8)]
        c = [lanes_of(a[s], j) for j in js]
        strip = a[s]
        rows, mult = [], [[None] * 8 for _ in range(8)]
        pivots = jnp.zeros((8, 128), F32)
        for q in range(8):
            pivot = row_of(c[q], q)
            over = 1.0 / pivot
            pivots = jnp.where(sub == q, pivot, pivots)
            below = jnp.where(sub > q, c[q], 0.0)
            strip = jnp.where(lane == js[q], jnp.where(sub == q, 1.0, 0.0), strip)
            row = row_of(strip, q) * over
            rows.append(jnp.where((lane <= js[q]) | (lane > js[7]), row, 0.0))
            for q2 in range(q + 1, 8):
                m = row_of(c[q2], q) * over
                mult[q][q2] = m
                c[q2] = c[q2] - below * m
            strip = strip - below * row
        a[s] = jnp.where(lane <= sub + 8 * s, strip, 0.0) * lax.rsqrt(pivots)
        kept = (lane < js[0]) | (lane > js[7])
        for t in range(s + 1, 16):
            ct = [lanes_of(a[t], j) for j in js]
            for q in range(8):
                for q2 in range(q + 1, 8):
                    ct[q2] = ct[q2] - ct[q] * mult[q][q2]
            value = jnp.where(kept, a[t], 0.0)
            for q in range(8):
                value = value - ct[q] * rows[q]
            a[t] = value
    return jnp.concatenate(a, axis=0)


def holders(place, mine, other, shifts):
    core, y, x = place[2], place[3], place[4]
    for refs, at_core in ((mine, core), (other, 1 - core)):
        for dx, dy, index, part in shifts:
            ref = refs[index] if part is None else refs[index].at[part]
            from_x, from_y = (x - dx) & 1, (y - dy) & 3
            middle = ((from_y + 1) >> 1) & 1
            yield ref, from_x * 8 + from_y * 2 + at_core, at_core + 2 * middle, from_x * 2 + (from_y >> 1)


def corner_kernel(place, panel_ref, lanes_ref, *refs):
    mine, other = refs[:4], refs[4:8]
    high_ref, low_ref, inv_ref, s_ref, raw_s, child_s, placed_s = refs[8:]
    n, b = PW // KB, KB
    row = place[0]
    slot_of = iota((8, 128), 1) >> 5
    for ref, holder, k, q in holders(place, mine, other, PLANE_SHIFTS):
        for block in range(PB):
            start = pl.multiple_of(block * BS + q * QUARTER, QUARTER)
            raw_s[k, pl.ds(start, QUARTER), :] = ref[(row - block) & 3, 0:QUARTER, :]
        lane_slot = holder & 3
        for block in range(2 * PB):
            at = QUARTER + (block // PB) * 8
            for half in range(2):
                value = ref[(row - block) & 3, at:at + 8, half * 128:(half + 1) * 128]
                for g in range(4):
                    start = (block * 2 + half) * 32 + g * 8
                    shifted = pltpu.roll(value, ((lane_slot - g) & 3) * 32, 1)
                    old = child_s[holder >> 2, start:start + 8, :]
                    child_s[holder >> 2, start:start + 8, :] = jnp.where(
                        slot_of == lane_slot, shifted, old
                    )
    child = jnp.concatenate([child_s[i] for i in range(4)], axis=1)
    child = 0.5 * (child + child.T)
    col_hot = as_hot(panel_ref[:, 0:1] == iota((512, PW), 1))
    placed_s[...] = sum(nn(part, col_hot) for part in split3(child))
    lanes = lanes_ref[0:1, :]
    raw = lambda i, j: raw_s[j // 2, i * b:(i + 1) * b, (j % 2) * b:(j % 2 + 1) * b]
    for i in range(n):
        row_hot = as_hot(iota((b, 512), 0) + i * b == lanes)
        added = sum(nn(row_hot, part) for part in split3(placed_s[:, :(i + 1) * b]))
        for j in range(i + 1):
            s_ref[i * b:(i + 1) * b, j * b:(j + 1) * b] = (
                0.5 * (raw(i, j) + raw(j, i).T) + added[:, j * b:(j + 1) * b]
            )
    for k in range(n):
        lo, hi = k * b, (k + 1) * b
        diag = factor_inverse(s_ref[lo:hi, lo:hi])
        if k < n - 1:
            below = nt(s_ref[hi:, lo:hi], diag, HIGHEST)
            s_ref[hi:, hi:hi + b] = s_ref[hi:, hi:hi + b] - nt(below, below[:b], HIGHEST)
        if k > 0:
            left = nn(diag, inv_ref[lo:hi, :lo], HIGHEST)
            inv_ref[lo:hi, :lo] = left
        inv_ref[lo:hi, lo:hi] = diag
        high_ref[lo:hi, :hi], low_ref[lo:hi, :hi] = split2(inv_ref[lo:hi, :hi])
        if k % 2 == 0:
            high_ref[lo:hi, hi:hi + b] = jnp.zeros((b, b), BF16)
            low_ref[lo:hi, hi:hi + b] = jnp.zeros((b, b), BF16)
        if k < n - 1:
            for j in range(k + 2, n):
                at = (j - k - 1) * b
                s_ref[j * b:, j * b:(j + 1) * b] = s_ref[j * b:, j * b:(j + 1) * b] - nt(
                    below[at:], below[at:at + b], HIGHEST
                )
            if k > 0:
                inv_ref[hi:, :lo] = inv_ref[hi:, :lo] - nn(below, left, HIGHEST)
            inv_ref[hi:, lo:hi] = -nn(below, diag, HIGHEST)


def corner_inverse(place, panel, lanes, mine, other):
    smem = pl.BlockSpec(memory_space=pltpu.SMEM)
    vmem = pl.BlockSpec(memory_space=pltpu.VMEM)
    return pl.pallas_call(
        corner_kernel,
        out_shape=(jax.ShapeDtypeStruct((PW, PW), BF16),) * 2,
        in_specs=[smem] + [vmem] * 10,
        out_specs=(vmem, vmem),
        scratch_shapes=[
            pltpu.VMEM((PW, PW), F32),
            pltpu.VMEM((PW, PW), F32),
            pltpu.VMEM((PB, PW, BS), F32),
            pltpu.VMEM((4, 512, 128), F32),
            pltpu.VMEM((512, PW), F32),
        ],
        compiler_params=pltpu.CompilerParams(vmem_limit_bytes=48 << 20),
        cost_estimate=pl.CostEstimate(
            flops=40_000_000_000, bytes_accessed=8 << 20, transcendentals=0
        ),
        name="corner_inverse",
    )(place, panel, lanes, *mine, *other)


def three_pass(a, b):
    return nt(a[0], b[0]) + nt(a[0], b[1]) + nt(a[1], b[0])


def schur_kernel(
    place, pattern, inv_h, inv_l, rows_ref, cols_ref, lanes_ref, panel_ref, landed_ref, held_ref, front_ref, *refs
):
    mine, other = refs[:4], refs[4:8]
    (out_ref, raw_s, col_h, col_l, row_h, row_l, row_f, child_s, child_p) = refs[8:]
    row, col = place[0], place[1]
    step = pl.program_id(0)
    per, lc = out_ref.shape[:2]

    def solve(raw, high_ref, low_ref, full_ref=None):
        raw = split2(raw)
        for j in range(PB):
            lo, deep = j * BS, (j + 1) * BS
            value = three_pass(
                (raw[0][:, :deep], raw[1][:, :deep]), (inv_h[lo:deep, :deep], inv_l[lo:deep, :deep])
            )
            high_ref[:, lo:deep], low_ref[:, lo:deep] = split2(value)
            if full_ref is not None:
                full_ref[:, lo:deep] = value

    @pl.when(step == 0)
    def _():
        col_hot = as_hot(panel_ref[:, 0:1] == iota((512, PW), 1))
        held_child = []
        for run in range(16):
            held_child.append(
                jnp.concatenate(
                    [
                        held_ref[run // 2, 384 + g * 8:392 + g * 8, (run % 2) * 128:(run % 2 + 1) * 128]
                        for g in range(4)
                    ],
                    axis=1,
                )
            )
        held_child = jnp.concatenate(held_child, axis=0)
        placed = split2(sum(nn(part, col_hot) for part in split2(held_child)))
        raw = []
        for k in range(PB):
            column = []
            for m in range(lc):
                for q in range(4):
                    at = HOLDER[k][q] * 24 + m * 8
                    column += [held_ref[r, at:at + 8, :] for r in range(8)]
            raw.append(jnp.concatenate(column, axis=0))
        raw = jnp.concatenate(raw, axis=1)
        row_hot = as_hot(iota((lc * BS, 128), 0) == col_place(lanes_ref[0:1, :]))
        solve(raw + sum(nn(row_hot, part) for part in placed), col_h, col_l)
        for ref, holder, k, q in holders(place, mine, other, PLANE_SHIFTS):
            child_s[pl.ds(pl.multiple_of(holder * 32, 32), 32), :] = ref[384:416, :]
        placed = sum(nn(part, col_hot) for part in split2(child_s[...].T))
        child_p[0], child_p[1] = split2(placed)

    for ref, holder, k, q in holders(place, mine, other, PLANE_SHIFTS):
        for h in range(per):
            start = pl.multiple_of(h * BS + q * QUARTER, QUARTER)
            at = pl.multiple_of((step * per + h) * QUARTER, QUARTER)
            raw_s[k, pl.ds(start, QUARTER), :] = ref[pl.ds(at, QUARTER), :]
    row_hot = as_hot(
        iota((per * BS, 256), 0) + step * (per * BS) == row_place(rows_ref[0:1, :])
    )
    raw_rows = jnp.concatenate([raw_s[k] for k in range(PB)], axis=1)
    raw_rows = raw_rows + nn(row_hot, child_p[0]) + nn(row_hot, child_p[1])
    solve(raw_rows, row_h, row_l, row_f)

    added = split3(sum(nt(row_hot, part) for part in split3(landed_ref[...])))
    for m in range(lc):
        col_hot = as_hot(col_place(cols_ref[:, 0:1]) == iota((128, BS), 1) + m * BS)
        e = sum(nn(part, col_hot) for part in added)
        block_col = m * 16 + col
        for h in range(per):
            block_row = (step * per + h) * 8 + row
            at = slice(h * BS, (h + 1) * BS)
            out_ref[h, m] = front_ref[h, m] + e[at]
            applied = (pattern[block_row, block_col] == 1) & (block_row >= PB) & (block_col >= PB)

            @pl.when(applied)
            def _():
                out_ref[h, m] = out_ref[h, m] - three_pass(
                    (row_h[at], row_l[at]),
                    (col_h[m * BS:(m + 1) * BS], col_l[m * BS:(m + 1) * BS]),
                )

    @pl.when(col < PB)
    def _():
        start = pl.multiple_of(jnp.minimum(col, PB - 1) * BS, BS)
        for h in range(per):
            out_ref[h, 0] = row_f[h * BS:(h + 1) * BS, pl.ds(start, BS)]


def schur_update(place, pattern, inverse, rows, cols, lanes, panel, landed, held, blocks, mine, other):
    lr, lc = blocks.shape[:2]
    per = 2
    smem = pl.BlockSpec(memory_space=pltpu.SMEM)
    whole = lambda x: pl.BlockSpec(x.shape, lambda l: (0,) * x.ndim)
    tile = pl.BlockSpec((per, lc, BS, BS), lambda l: (l, 0, 0, 0))
    return pl.pallas_call(
        schur_kernel,
        grid=(lr // per,),
        out_shape=jax.ShapeDtypeStruct(blocks.shape, F32),
        in_specs=[smem, smem]
        + [whole(x) for x in (*inverse, rows, cols, lanes, panel, landed, held)]
        + [tile]
        + [whole(x) for x in (*mine, *other)],
        out_specs=tile,
        scratch_shapes=[
            pltpu.VMEM((PB, per * BS, BS), F32),
            pltpu.VMEM((lc * BS, PW), BF16),
            pltpu.VMEM((lc * BS, PW), BF16),
            pltpu.VMEM((per * BS, PW), BF16),
            pltpu.VMEM((per * BS, PW), BF16),
            pltpu.VMEM((per * BS, PW), F32),
            pltpu.VMEM((512, 256), F32),
            pltpu.VMEM((2, 256, PW), BF16),
        ],
        compiler_params=pltpu.CompilerParams(vmem_limit_bytes=60 << 20),
        cost_estimate=pl.CostEstimate(
            flops=16_000_000_000, bytes_accessed=24 << 20, transcendentals=0
        ),
        name="schur_update",
    )(place, pattern, *inverse, rows, cols, lanes, panel, landed, held, blocks, *mine, *other)


def after(x, *first):
    return lax.optimization_barrier((x,) + first)[0]


def scatter_quarters(quarters, col):
    got = jnp.where(col < PB, quarters[0], 0.0)
    for q in range(1, 4):
        got = got + lax.ppermute(quarters[q], "col", [(k, HOLDER[k][q]) for k in range(PB)])
    return got


def shift_plane(x, dx, dy):
    pairs = []
    for c in range(16):
        at_x, at_y, core = c // 8, (c // 2) % 4, c % 2
        pairs.append((c, ((at_x + dx) % 2) * 8 + ((at_y + dy) % 4) * 2 + core))
    return lax.ppermute(x, "col", pairs)


def gather_plane(piece):
    both = jnp.stack([piece, shift_plane(piece, 1, 0)])
    return [both] + [shift_plane(both, 0, dy) for dy in (1, 2, 3)]


def swap_cores(pieces):
    return [lax.ppermute(x, "col", [(c, c ^ 1) for c in range(16)]) for x in pieces]


def shift_row(x, d):
    return lax.ppermute(x, "row", [(z, (z + d) % 8) for z in range(8)])


def per_device(front, child_update, child_map, pattern):
    row = lax.axis_index("row")
    col = lax.axis_index("col")
    place = jnp.stack([row, col, col % 2, (col // 2) % 4, col // 8]).astype(jnp.int32)
    blocks = front[0].transpose(0, 2, 1, 3)
    lr, lc = blocks.shape[:2]
    msg, corner_child, part, rows, cols, lanes, panel_sub, panel_lanes = pack(
        place, child_map[0].reshape(16, 128), child_update[0]
    )

    first = blocks[0, 0]
    first = scatter_quarters([first[q * QUARTER:(q + 1) * QUARTER] for q in range(4)], col)
    corner = jnp.concatenate([first, corner_child], axis=0)
    from_far = shift_row(corner, 4)
    low = jnp.where(row < PB, corner, from_far)
    high = jnp.where(row < PB, from_far, corner)
    corner = jnp.concatenate([low, high[QUARTER:]], axis=0)
    corner = jnp.stack([corner, shift_row(corner, 1), shift_row(corner, 2), shift_row(corner, 7)])
    corner_mine = gather_plane(corner)
    over_planes = corner
    corner_other = swap_cores(corner_mine)
    inverse = corner_inverse(place, panel_sub, panel_lanes, corner_mine, corner_other)

    lead = after(blocks[:, 0], first).reshape(lr, 4, QUARTER, BS)
    own = scatter_quarters([lead[:, q] for q in range(4)], col)
    sent = own.reshape(lr, 8, 8, BS).transpose(1, 0, 2, 3).reshape(8, lr * 8, BS)
    sent = after(jnp.concatenate([sent, msg], axis=1), over_planes)
    sent = lax.all_to_all(sent, "row", split_axis=0, concat_axis=0, tiled=True)
    turned = turn(sent[:, lr * 8:])
    strips = sent[:, :lr * 8].reshape(8, lc, 2, 8, BS).transpose(2, 0, 1, 3, 4)
    sent = jnp.concatenate(
        [strips.reshape(16, lc * 8, BS), turned.reshape(16, 8, BS), part], axis=1
    )
    sent = after(sent, corner_mine[1])
    sent = lax.all_to_all(sent, "col", split_axis=0, concat_axis=0, tiled=True)
    landed = sent[:, lc * 8:lc * 8 + 8].reshape(128, 256)
    held = jnp.concatenate(
        [
            sent[:, :lc * 8].reshape(16 * lc * 8, BS),
            sent[:, lc * 8 + 8:].reshape(4, 4, 8, BS).sum(1).reshape(32, BS),
        ],
        axis=0,
    )
    held = lax.all_gather(held, "row", axis=0, tiled=False)

    own = jnp.concatenate([own.reshape(lr * QUARTER, BS), turned[:32]], axis=0)
    panel_mine = gather_plane(own)
    panel_other = swap_cores(panel_mine[:1] + [after(x, inverse[0]) for x in panel_mine[1:]])
    out = schur_update(
        place, pattern[0], inverse, rows, cols, lanes, panel_sub, landed, held, blocks,
        panel_mine, panel_other,
    )
    return out.transpose(0, 2, 1, 3)[None]


def solution(mesh):
    placed = (
        P("front", None, "row", None, "col"),
        P("front", "row", "col"),
        P("front", None),
        P("front", None, None),
    )
    return jax.shard_map(
        per_device,
        mesh=mesh,
        in_specs=placed,
        out_specs=P("front", None, "row", None, "col"),
        check_vma=False,
    )
```
